32 devices in a mesh: groups: 2 (over y), rows: 4 (over x, core), cols: 4 (over z).
Axes of the slice: x: 2, y: 2, z: 4, core: 2. Of those that a mesh axis runs over, the one named last changes fastest.
Arguments:
- features: bfloat16 [4096, 256], P(('groups', 'rows', 'cols')), parts along dimension 0, may hold values from -6 to 6
- degree: int32 [4096], P(('groups', 'rows', 'cols')), parts along dimension 0, may hold values from 1 to 8
- weight: bfloat16 [256, 256], replicated, may hold values from -0.375 to 0.375
- tile_index: int32 [8, 4, 2, 8], P(('groups', 'rows'), 'cols'), parts along dimension 0, may hold values from 0 to 3, as said below
- tile_values: bfloat16 [8, 4, 8, 128, 128], P(('groups', 'rows'), 'cols'), parts along dimension 0, may hold values from -0.25 to 0.25
- tile_count: int32 [8, 4], P(('groups', 'rows'), 'cols'), parts along dimension 0, may hold values from 1 to 8, as said below
- cotangent: bfloat16 [4096, 256], P(('groups', 'rows', 'cols')), parts along dimension 0, may hold values from -6 to 6
Outputs:
- activated: bfloat16 [4096, 256], P(('groups', 'rows', 'cols')), parts along dimension 0
- input_grad: bfloat16 [4096, 256], P(('groups', 'rows', 'cols')), parts along dimension 0
- weight_grad: float32 [512, 256], P('groups'), parts along dimension 0
The draws below stay inside these ranges and needn't reach their ends.
There are 2 independent parts, one for each index of `groups`. The reference program is written for one: setup_inputs(seed, part) draws one part's arguments, and reference() takes and returns one part's arrays. A program takes and returns all parts, laid end to end along the dimension named above; an argument that names none is the same for every part. Nothing has to cross between parts.
Inputs may be any that keep to these rules, and one draw needn't show every extreme that they name: `tile_index`: tile rows lie below 4 and tile columns below 4; slots at or past a block's tile_count hold no tile, whatever they contain. `tile_count`: some block uses all 8 slots.
All inputs are finite; a program needn't handle non-finite values.
Results may differ from the reference program's by a relative error of at most 0.015.
Values may be sent and summed in bfloat16 or wider, within the bound.
No kernel may reach another device: no remote copies, remote signals or barrier semaphores. Data moves between devices by JAX's collectives and lax.ppermute only.
A program may use at most 64 MiB of HBM per device.

```python
import jax
import jax.numpy as jnp
from jax import lax

F = 256
TILE = 128
ROWS_DEV = 128
TILES = 8
NODES = 2048
ROW_TILES = 4
COL_TILES = 4
N_ROWS = 4
N_COLS = 4


def draw_tile_index(key, part):
    key = jax.random.fold_in(key, 11)
    row_key, col_key = jax.random.split(key)
    row_part = jax.random.randint(row_key, (N_ROWS, N_COLS, 1, TILES), 0, ROW_TILES)
    col_part = jax.random.randint(col_key, (N_ROWS, N_COLS, 1, TILES), 0, COL_TILES)
    return jnp.concatenate([row_part, col_part], axis=2).astype(jnp.int32)


def draw_tile_count(key, part):
    key = jax.random.fold_in(key, 23)
    level_key, peak_key = jax.random.split(key)
    flat_levels = jax.random.randint(level_key, (N_ROWS * N_COLS,), 0, 4)
    peak_slot = jax.random.randint(peak_key, (), 0, N_ROWS * N_COLS)
    flat_levels = jnp.where(jnp.arange(N_ROWS * N_COLS) == peak_slot, 0, flat_levels)
    counts = jnp.maximum(TILES // jnp.left_shift(1, flat_levels), 1)
    return counts.reshape(N_ROWS, N_COLS).astype(jnp.int32)


def touch_ends(array, rng, least, largest):
    shape = array.shape
    place = [jax.random.randint(jax.random.fold_in(rng, axis), (), 0, shape[axis]) for axis in range(len(shape))]
    array = array.at[tuple(place)].set(least)
    longest = shape.index(max(shape))
    place[longest] = (place[longest] + 1) % shape[longest]
    return array.at[tuple(place)].set(largest)


def shard_levels(stream_key, extent, shards, smallest, high):
    factor_of = 1.0
    for axis_at, shards_of in shards:
        heights = jax.random.uniform(jax.random.fold_in(jax.random.fold_in(stream_key, 6), axis_at), (shards_of,), jnp.float32, smallest / len(shards), high / len(shards))
        factor_of = factor_of * jnp.repeat(jnp.exp(heights), extent[axis_at] // shards_of).reshape((-1,) + (1,) * (len(extent) - 1 - axis_at))
    return factor_of


def centred(rng, dims, scale, bound, shards=(), kind=jnp.bfloat16):
    result = scale * jax.random.normal(rng, dims, jnp.float32)
    if shards:
        result = result * shard_levels(rng, dims, shards, -0.22, 0.18)
    return jnp.clip(result, -bound, bound).astype(kind)


def setup_inputs(seed: int = 0, part: int = 0) -> dict:
    key_of = jax.random.split(jax.random.key(seed), 8)
    part_keys = jax.random.split(jax.random.fold_in(key_of[7], part), 8)
    features = centred(part_keys[0], (NODES, F), 1.0, 6.0, ((0, 16),))
    degree = touch_ends(jax.random.randint(part_keys[1], (NODES,), 1, 9), jax.random.fold_in(part_keys[1], 1), 1, 8).astype(jnp.int32)
    weight = centred(key_of[2], (F, F), F ** -0.5, 0.375)
    tile_index = draw_tile_index(jax.random.fold_in(jax.random.fold_in(key_of[7], part), 71), part)
    tile_values = centred(part_keys[4], (N_ROWS, N_COLS, TILES, TILE, TILE), (TILES * 8192 // ROWS_DEV) ** -0.5, 0.25, ((0, 4), (1, 4)))
    tile_count = draw_tile_count(jax.random.fold_in(jax.random.fold_in(key_of[7], part), 71), part)
    cotangent = centred(part_keys[6], (NODES, F), 1.0, 6.0, ((0, 16),))
    return dict(features=features, degree=degree, weight=weight, tile_index=tile_index, tile_values=tile_values, tile_count=tile_count, cotangent=cotangent)


def apply_tiles(values, take_idx, put_idx, used_count, source, out_tiles, transposed):
    width = source.shape[1]
    tile_total = values.shape[0]
    source_tiles = source.reshape(-1, 128, width)
    picked = jnp.take(source_tiles, take_idx, axis=0)
    einsum_form = 'kba,kbf->kaf' if transposed else 'kab,kbf->kaf'
    products = jnp.einsum(einsum_form, values.astype(jnp.float32), picked.astype(jnp.float32), precision=lax.Precision.HIGHEST)
    live_mask = (jnp.arange(tile_total, dtype=jnp.int32) < used_count).astype(jnp.float32)
    onehot = (put_idx[None, :] == jnp.arange(out_tiles, dtype=jnp.int32)[:, None]).astype(jnp.float32) * live_mask[None, :]
    placed = jnp.einsum('rk,kaf->raf', onehot, products, precision=lax.Precision.HIGHEST)
    return placed.reshape(out_tiles * 128, width)

def reference(features, degree, weight, tile_index, tile_values, tile_count, cotangent):
    width = features.shape[1]
    inv_root = lax.rsqrt(degree.astype(jnp.float32))
    scaled = (inv_root[:, None] * features.astype(jnp.float32)).astype(jnp.bfloat16)
    scaled_grid = scaled.reshape(N_ROWS, N_COLS, ROWS_DEV, width)

    def forward_row(row_block):

        def add_block(total, col_block):
            panel = lax.dynamic_index_in_dim(scaled_grid, col_block, 1, keepdims=False).reshape(N_ROWS * ROWS_DEV, width)
            coords = tile_index[row_block, col_block]
            partial_value = apply_tiles(tile_values[row_block, col_block], coords[1], coords[0], tile_count[row_block, col_block], panel, ROW_TILES, False)
            rounded = lax.optimization_barrier(partial_value.astype(jnp.bfloat16))
            return (total + rounded.astype(jnp.float32), None)
        start = jnp.zeros((N_COLS * ROWS_DEV, width), jnp.float32)
        total, unused = lax.scan(add_block, start, jnp.arange(N_COLS, dtype=jnp.int32))
        return total
    row_sums = lax.map(forward_row, jnp.arange(N_ROWS, dtype=jnp.int32)).reshape(NODES, width)
    aggregated = (inv_root[:, None] * row_sums).astype(jnp.bfloat16)
    pre_act = jnp.dot(aggregated, weight, preferred_element_type=jnp.float32)
    sig = jax.nn.sigmoid(pre_act)
    activated = (pre_act * sig).astype(jnp.bfloat16)
    act_grad = (cotangent.astype(jnp.float32) * sig * (1.0 + pre_act * (1.0 - sig))).astype(jnp.bfloat16)
    back_pre = lax.dot_general(act_grad, weight, (((1,), (1,)), ((), ())), preferred_element_type=jnp.float32)
    spread = (inv_root[:, None] * back_pre).astype(jnp.bfloat16)
    spread_rows = spread.reshape(N_ROWS, N_COLS * ROWS_DEV, width)

    def backward_col(col_block):

        def add_block(total, row_block):
            coords = tile_index[row_block, col_block]
            panel = lax.dynamic_index_in_dim(spread_rows, row_block, 0, keepdims=False)
            partial_value = apply_tiles(tile_values[row_block, col_block], coords[0], coords[1], tile_count[row_block, col_block], panel, COL_TILES, True)
            return (total + partial_value, None)
        start = jnp.zeros((N_ROWS * ROWS_DEV, width), jnp.float32)
        total, unused = lax.scan(add_block, start, jnp.arange(N_ROWS, dtype=jnp.int32))
        return total
    column_sums = lax.map(backward_col, jnp.arange(N_COLS, dtype=jnp.int32))
    column_sums = column_sums.reshape(N_COLS, N_ROWS, ROWS_DEV, width).transpose(1, 0, 2, 3).reshape(NODES, width)
    input_grad = (inv_root[:, None] * column_sums).astype(jnp.bfloat16)
    weight_term = lax.dot_general(aggregated, act_grad, (((0,), (0,)), ((), ())), preferred_element_type=jnp.float32)
    weight_grad = weight_term / jnp.sqrt(jnp.float32(NODES))
    return (activated, input_grad, weight_grad)
```

```python
import functools
import math

import jax
import jax.numpy as jnp
from jax import lax
from jax.experimental import pallas as pl
from jax.experimental.pallas import tpu as pltpu
from jax.sharding import PartitionSpec as P

TILE = 128
DEG_ROWS = 16
BF16 = jnp.bfloat16
F32 = jnp.float32


def reverse_bits(value, bits):
    out = value & 0
    for bit in range(bits):
        out = out | (((value >> bit) & 1) << (bits - 1 - bit))
    return out


def doubling_masks(size):
    return [2 ** (step + 1) - 1 for step in range(size.bit_length() - 1)]


def slot_offsets(masks):
    offsets = [0]
    for mask in masks:
        offsets = offsets + [offset ^ mask for offset in offsets]
    return offsets


def row_scale(degree_lanes):
    spread = jnp.broadcast_to(degree_lanes.astype(F32), (TILE, TILE))
    return lax.rsqrt(spread.T)


def wide(scale, width):
    return jnp.concatenate([scale] * (width // TILE), axis=1)


def tile_loop(idx_ref, cnt_ref, body):
    tiles = idx_ref.shape[-1]
    used = cnt_ref[0, 0]
    for slot in range(tiles):
        live = slot < used
        row = jnp.where(live, idx_ref[0, 0, 0, slot], 0)
        col = jnp.where(live, idx_ref[0, 0, 1, slot], 0)
        body(slot, live, row, col)


def rows_at(block, rows=TILE):
    return pl.ds(pl.multiple_of(block * rows, rows), rows)


def scale_kernel(deg_ref, x_ref, out_ref):
    scale = row_scale(deg_ref[...].reshape(1, TILE))
    out_ref[...] = (wide(scale, x_ref.shape[1]) * x_ref[...].astype(F32)).astype(BF16)


def forward_kernel(n_rows, n_cols, idx_ref, cnt_ref, values_ref, deg_ref, cot_ref, *rest):
    blocks, (out_ref, panel, acc) = rest[:n_rows], rest[n_rows:]
    me = lax.axis_index("rows")
    for shift, block in enumerate(blocks):
        panel[lax.rem(me - shift + n_rows, n_rows)] = block[...]
    acc[...] = jnp.zeros_like(acc)

    def body(slot, live, row, col):
        tile = jnp.where(live, values_ref[0, 0, slot], jnp.zeros((TILE, TILE), BF16))
        acc[rows_at(row), :] += jnp.dot(tile, panel[col], preferred_element_type=F32)

    tile_loop(idx_ref, cnt_ref, body)
    panel_rows = n_cols * TILE
    out_ref[:panel_rows] = acc[...].astype(BF16)
    out_ref[panel_rows : panel_rows + TILE] = cot_ref[...]
    degree = deg_ref[...].reshape(1, TILE).astype(F32)
    out_ref[panel_rows + TILE :, :TILE] = jnp.broadcast_to(degree, (DEG_ROWS, TILE)).astype(BF16)


def merge_kernel(panel_rows, own_ref, got_ref, out_ref):
    out_ref[:panel_rows] = (
        own_ref[:panel_rows].astype(F32) + got_ref[:panel_rows].astype(F32)
    ).astype(BF16)
    extra = own_ref.shape[0] - panel_rows
    out_ref[panel_rows : panel_rows + extra] = own_ref[panel_rows:]
    out_ref[panel_rows + extra :] = got_ref[panel_rows:]


def middle_kernel(
    n_rows, n_cols, idx_ref, cnt_ref, values_ref, own_ref, got_ref, weight_ref,
    act_ref, keep_ref, send_ref, spread, hidden, weight_acc,
):
    width = weight_ref.shape[0]
    panel_rows = n_cols * TILE
    extra = own_ref.shape[0] - panel_rows
    per_side = extra // (TILE + DEG_ROWS)
    row, col = lax.axis_index("rows"), lax.axis_index("cols")
    odd = lax.rem(row, 2) == 1
    masks = doubling_masks(n_cols)
    even_offsets, odd_offsets = slot_offsets(masks), slot_offsets(masks[::-1])
    weight = weight_ref[...]
    weight_acc[...] = jnp.zeros_like(weight_acc)
    hidden[...] = jnp.zeros_like(hidden)
    for slot in range(n_cols):
        block = col ^ jnp.where(odd, odd_offsets[slot], even_offsets[slot])
        side = own_ref if slot < per_side else got_ref
        at = panel_rows + (slot % per_side) * (TILE + DEG_ROWS)
        here = rows_at(block)
        sums = own_ref[here, :].astype(F32) + got_ref[here, :].astype(F32)
        scale = wide(row_scale(side[at + TILE : at + TILE + 1, :TILE]), width)
        aggregated = (scale * sums).astype(BF16)
        pre_act = jnp.dot(aggregated, weight, preferred_element_type=F32)
        sig = 1.0 / (1.0 + jnp.exp(-pre_act))
        if slot == 0:
            act_ref[...] = (pre_act * sig).astype(BF16)
        grad = side[at : at + TILE, :].astype(F32) * sig * (1.0 + pre_act * (1.0 - sig))
        spread[block] = (scale * grad).astype(BF16)
        weight_acc[...] += lax.dot_general(
            aggregated, grad.astype(BF16), (((0,), (0,)), ((), ())), preferred_element_type=F32
        )

    bits = n_rows.bit_length() - 1

    def body(slot, live, tile_row, tile_col):
        tile = jnp.where(live, values_ref[0, 0, slot], jnp.zeros((TILE, TILE), BF16))
        place = reverse_bits(tile_col ^ row, bits)
        hidden[rows_at(place), :] += lax.dot_general(
            tile, spread[tile_row], (((0,), (0,)), ((), ())), preferred_element_type=F32
        )

    tile_loop(idx_ref, cnt_ref, body)
    half = n_rows * TILE // 2
    keep_ref[...] = hidden[:half]
    send_ref[:half] = hidden[half:].astype(BF16)
    send_ref[half:] = weight_acc[...].astype(BF16)


def fold_kernel(keep_ref, sent_ref, got_ref, keep_out, send_out):
    rows = keep_ref.shape[0]
    half = rows // 2
    keep_out[...] = keep_ref[:half] + got_ref[:half].astype(F32)
    send_out[:half] = (keep_ref[half:] + got_ref[half:rows].astype(F32)).astype(BF16)
    send_out[half:] = (sent_ref[rows:].astype(F32) + got_ref[rows:].astype(F32)).astype(BF16)


def last_kernel(weight_scale, deg_ref, weight_ref, keep_ref, sent_ref, got_ref, grad_ref, wgrad_ref):
    rows = keep_ref.shape[0]
    hidden = (keep_ref[...] + got_ref[:rows].astype(F32)).astype(BF16)
    back = lax.dot_general(
        hidden, weight_ref[...], (((1,), (1,)), ((), ())), preferred_element_type=F32
    )
    scale = wide(row_scale(deg_ref[...].reshape(1, TILE)), back.shape[1])
    grad_ref[...] = (scale * back).astype(BF16)
    wgrad_ref[...] = (sent_ref[rows:].astype(F32) + got_ref[rows:].astype(F32)) * weight_scale


def call(body, out_shapes, places, scratch=()):
    return pl.pallas_call(
        body,
        out_shape=out_shapes,
        in_specs=[pl.BlockSpec(memory_space=place) for place in places],
        scratch_shapes=list(scratch),
        compiler_params=pltpu.CompilerParams(vmem_limit_bytes=24 * 1024 * 1024),
    )


def shards(features, degree, weight, tile_index, tile_values, tile_count, cotangent):
    width = features.shape[1]
    n_rows = lax.axis_size("rows")
    n_cols = lax.axis_size("cols")
    shape = jax.ShapeDtypeStruct
    smem, vmem = pltpu.SMEM, pltpu.VMEM
    panel_rows = n_cols * TILE

    scaled = call(scale_kernel, shape((TILE, width), BF16), [vmem, vmem])(degree, features)
    blocks = [scaled] + [None] * (n_rows - 1)
    for shift in reversed(range(1, n_rows)):
        blocks[shift] = lax.ppermute(
            scaled, "rows", [(i, (i + shift) % n_rows) for i in range(n_rows)]
        )
    part = call(
        functools.partial(forward_kernel, n_rows, n_cols),
        shape((panel_rows + TILE + DEG_ROWS, width), BF16),
        [smem, smem] + [vmem] * (3 + n_rows),
        [vmem((n_rows, TILE, width), BF16), vmem((panel_rows, width), F32)],
    )(tile_index, tile_count, tile_values, degree, cotangent, *blocks)

    masks = doubling_masks(n_cols)
    for step in range(len(masks)):
        pairs = []
        for i in range(n_rows):
            mask = masks[::-1][step] if i % 2 else masks[step]
            pairs += [(i * n_cols + j, i * n_cols + (j ^ mask)) for j in range(n_cols)]
        got = lax.ppermute(part, ("rows", "cols"), pairs)
        if step + 1 < len(masks):
            rows = 2 * part.shape[0] - panel_rows
            part = call(
                functools.partial(merge_kernel, panel_rows), shape((rows, width), BF16), [vmem] * 2
            )(part, got)
    half = n_rows * TILE // 2
    activated, keep, send = call(
        functools.partial(middle_kernel, n_rows, n_cols),
        (
            shape((TILE, width), BF16),
            shape((half, width), F32),
            shape((half + width, width), BF16),
        ),
        [smem, smem] + [vmem] * 4,
        [
            vmem((n_cols, TILE, width), BF16),
            vmem((n_rows * TILE, width), F32),
            vmem((width, width), F32),
        ],
    )(tile_index, tile_count, tile_values, part, got, weight)
    mask = 1
    while True:
        got = lax.ppermute(send, "rows", [(i, i ^ mask) for i in range(n_rows)])
        mask *= 2
        if mask == n_rows:
            break
        half = keep.shape[0] // 2
        keep, send = call(
            fold_kernel, (shape((half, width), F32), shape((half + width, width), BF16)), [vmem] * 3
        )(keep, send, got)
    weight_scale = 1.0 / math.sqrt(TILE * n_rows * n_cols)
    input_grad, weight_grad = call(
        functools.partial(last_kernel, weight_scale),
        (shape((TILE, width), BF16), shape((width, width), F32)),
        [vmem] * 5,
    )(degree, weight, keep, send, got)
    return (activated, input_grad, weight_grad)


def solution(mesh):
    placed = (
        P(("groups", "rows", "cols"), None),
        P(("groups", "rows", "cols")),
        P(),
        P(("groups", "rows"), "cols", None, None),
        P(("groups", "rows"), "cols", None, None, None),
        P(("groups", "rows"), "cols"),
        P(("groups", "rows", "cols"), None),
    )
    return jax.shard_map(
        shards,
        mesh=mesh,
        in_specs=placed,
        out_specs=(
            P(("groups", "rows", "cols"), None),
            P(("groups", "rows", "cols"), None),
            P("groups", None),
        ),
        check_vma=False,
    )
```

```python
import functools
import math

import jax
import jax.numpy as jnp
from jax import lax
from jax.experimental import pallas as pl
from jax.experimental.pallas import tpu as pltpu
from jax.sharding import PartitionSpec as P

TILE = 128
DEG_ROWS = 16
BF16 = jnp.bfloat16
F32 = jnp.float32


def reverse_bits(value, bits):
    out = value & 0
    for bit in range(bits):
        out = out | (((value >> bit) & 1) << (bits - 1 - bit))
    return out


def row_scale(degree_lanes):
    spread = jnp.broadcast_to(degree_lanes.astype(F32), (TILE, TILE))
    return lax.rsqrt(spread.T)


def wide(scale, width):
    return jnp.concatenate([scale] * (width // TILE), axis=1)


def tile_loop(idx_ref, row_limit, col_limit, body):
    for slot in range(idx_ref.shape[-1]):
        row = jnp.clip(idx_ref[0, 0, 0, slot], 0, row_limit - 1)
        col = jnp.clip(idx_ref[0, 0, 1, slot], 0, col_limit - 1)
        body(slot, row, col)


def rows_at(block, rows=TILE):
    return pl.ds(pl.multiple_of(block * rows, rows), rows)


def scale_kernel(deg_ref, x_ref, out_ref):
    scale = wide(row_scale(deg_ref[...].reshape(1, TILE)), x_ref.shape[1])
    out_ref[...] = (scale * x_ref[...].astype(F32)).astype(BF16)


def extra_kernel(deg_ref, cot_ref, extra_ref):
    extra_ref[:TILE] = cot_ref[...]
    degree = jnp.broadcast_to(deg_ref[...].reshape(1, TILE).astype(F32), (DEG_ROWS, TILE))
    extra_ref[TILE:] = wide(degree, cot_ref.shape[1]).astype(BF16)


def tiles_kernel(cnt_ref, values_ref, tiles_ref, flipped_ref):
    used = jnp.broadcast_to(cnt_ref[...], (TILE, TILE))
    for slot in range(values_ref.shape[2]):
        tile = jnp.where(slot < used, values_ref[0, 0, slot].astype(F32), 0.0).astype(BF16)
        tiles_ref[slot] = tile
        flipped_ref[slot] = tile.T


def forward_kernel(n_rows, n_cols, idx_ref, tiles_ref, *rest):
    blocks, outs, (panel, acc) = rest[:n_rows], rest[n_rows : n_rows + n_cols], rest[n_rows + n_cols :]
    me, col_me = lax.axis_index("rows"), lax.axis_index("cols")
    for shift, block in enumerate(blocks):
        panel[me ^ shift] = block[...]
    acc[...] = jnp.zeros_like(acc)

    def body(slot, row, col):
        acc[rows_at(row), :] += jnp.dot(
            tiles_ref[slot], panel[col], preferred_element_type=F32
        )

    tile_loop(idx_ref, n_cols, n_rows, body)
    for shift, out in enumerate(outs):
        out[...] = acc[rows_at(col_me ^ shift), :].astype(BF16)


def own_rows_kernel(deg_ref, *rest):
    blocks, out_ref = rest[:-1], rest[-1]
    sums = blocks[0][...].astype(F32)
    for block in blocks[1:]:
        sums = sums + block[...].astype(F32)
    scale = wide(row_scale(deg_ref[...].reshape(1, TILE)), sums.shape[1])
    out_ref[...] = (scale * sums).astype(BF16)


def middle_kernel(n_cols, weight_ref, *rest):
    panels, extras = rest[:n_cols], rest[n_cols : 2 * n_cols]
    act_ref, spread_ref, term_keep, term_send, term = rest[2 * n_cols :]
    width = weight_ref.shape[0]
    col = lax.axis_index("cols")
    weight = weight_ref[...]
    term[...] = jnp.zeros_like(term)
    for shift in range(n_cols):
        extra = extras[shift]
        scale = wide(row_scale(extra[TILE : TILE + 1, :TILE]), width)
        aggregated = panels[shift][...]
        pre_act = jnp.dot(aggregated, weight, preferred_element_type=F32)
        sig = 1.0 / (1.0 + jnp.exp(-pre_act))
        if shift == 0:
            act_ref[...] = (pre_act * sig).astype(BF16)
        grad = extra[:TILE, :].astype(F32) * sig * (1.0 + pre_act * (1.0 - sig))
        spread_ref[col ^ shift] = (scale * grad).astype(BF16)
        term[...] += lax.dot_general(
            aggregated, grad.astype(BF16), (((0,), (0,)), ((), ())), preferred_element_type=F32
        )
    side = lax.rem(lax.axis_index("rows"), 2)
    half = width // 2
    term_keep[...] = term[rows_at(side, half), :]
    term_send[...] = term[rows_at(1 - side, half), :].astype(BF16)


def back_kernel(n_rows, n_cols, idx_ref, flipped_ref, spread_ref, keep_ref, send_ref, hidden):
    row = lax.axis_index("rows")
    hidden[...] = jnp.zeros_like(hidden)
    bits = n_rows.bit_length() - 1

    def body(slot, tile_row, tile_col):
        place = reverse_bits(tile_col ^ row, bits)
        hidden[rows_at(place), :] += jnp.dot(
            flipped_ref[slot], spread_ref[tile_row], preferred_element_type=F32
        )

    tile_loop(idx_ref, n_cols, n_rows, body)
    half = n_rows * TILE // 2
    keep_ref[...] = hidden[:half]
    send_ref[...] = hidden[half:].astype(BF16)


def fold_kernel(keep_ref, got_ref, keep_out, send_out):
    half = keep_ref.shape[0] // 2
    keep_out[...] = keep_ref[:half] + got_ref[:half].astype(F32)
    send_out[...] = (keep_ref[half:] + got_ref[half:].astype(F32)).astype(BF16)


def add_kernel(scale, own_ref, got_ref, out_ref):
    total = own_ref[...].astype(F32) + got_ref[...].astype(F32)
    out_ref[...] = (total * scale).astype(out_ref.dtype)


def join_kernel(own_ref, got_ref, out_ref):
    half = own_ref.shape[0]
    side = lax.rem(lax.axis_index("rows"), 2)
    out_ref[rows_at(side, half), :] = own_ref[...]
    out_ref[rows_at(1 - side, half), :] = got_ref[...]


def last_kernel(deg_ref, weight_ref, keep_ref, got_ref, grad_ref):
    hidden = (keep_ref[...] + got_ref[...].astype(F32)).astype(BF16)
    back = lax.dot_general(
        hidden, weight_ref[...], (((1,), (1,)), ((), ())), preferred_element_type=F32
    )
    scale = wide(row_scale(deg_ref[...].reshape(1, TILE)), back.shape[1])
    grad_ref[...] = (scale * back).astype(BF16)


def call(body, out_shapes, places, scratch=(), cost=None):
    return pl.pallas_call(
        body,
        out_shape=out_shapes,
        in_specs=[pl.BlockSpec(memory_space=place) for place in places],
        scratch_shapes=list(scratch),
        cost_estimate=cost,
        compiler_params=pltpu.CompilerParams(vmem_limit_bytes=24 * 1024 * 1024),
    )


def shards(features, degree, weight, tile_index, tile_values, tile_count, cotangent):
    width = features.shape[1]
    n_rows = lax.axis_size("rows")
    n_cols = lax.axis_size("cols")
    shape = jax.ShapeDtypeStruct
    smem, vmem = pltpu.SMEM, pltpu.VMEM
    tiles = tile_values.shape[2]

    def shifted(block, axis, size):
        got = [block] + [None] * (size - 1)
        for shift in reversed(range(1, size)):
            source = block[shift] if isinstance(block, (list, tuple)) else block
            got[shift] = lax.ppermute(source, axis, [(i, i ^ shift) for i in range(size)])
        if isinstance(block, (list, tuple)):
            got[0] = block[0]
        return got

    block_shape = shape((TILE, width), BF16)
    square = shape((tiles, TILE, TILE), BF16)
    slow = pl.CostEstimate(flops=10**10, bytes_accessed=10**6, transcendentals=0)
    scaled = call(scale_kernel, block_shape, [vmem] * 2, cost=slow)(degree, features)
    extra = call(extra_kernel, shape((TILE + DEG_ROWS, width), BF16), [vmem] * 2)(degree, cotangent)
    live_tiles, flipped = call(tiles_kernel, (square, square), [vmem] * 2)(tile_count, tile_values)
    blocks = shifted(scaled, "rows", n_rows)
    extras = shifted(extra, "cols", n_cols)
    parts = call(
        functools.partial(forward_kernel, n_rows, n_cols),
        [block_shape] * n_cols,
        [smem] + [vmem] * (1 + n_rows),
        [vmem((n_rows, TILE, width), BF16), vmem((n_cols * TILE, width), F32)],
        pl.CostEstimate(flops=2 * 10**10, bytes_accessed=10**6, transcendentals=0),
    )(tile_index, live_tiles, *blocks)
    sums = shifted(parts, "cols", n_cols)
    sums, extras = lax.optimization_barrier((sums, extras))
    aggregated = call(own_rows_kernel, block_shape, [vmem] * (1 + n_cols))(degree, *sums)
    panels = shifted(aggregated, "cols", n_cols)
    term_shape = shape((width // 2, width), BF16)
    activated, spread, term, term_send = call(
        functools.partial(middle_kernel, n_cols),
        (
            block_shape,
            shape((n_cols, TILE, width), BF16),
            shape(term_shape.shape, F32),
            term_shape,
        ),
        [vmem] * (1 + 2 * n_cols),
        [vmem((width, width), F32)],
    )(weight, *panels, *extras)
    half = n_rows * TILE // 2
    keep, send = call(
        functools.partial(back_kernel, n_rows, n_cols),
        (shape((half, width), F32), shape((half, width), BF16)),
        [smem] + [vmem] * 2,
        [vmem((n_rows * TILE, width), F32)],
    )(tile_index, flipped, spread)

    def partner(block, mask):
        return lax.ppermute(block, "rows", [(i, i ^ mask) for i in range(n_rows)])

    def add(dtype, scale, own, got):
        return call(
            functools.partial(add_kernel, scale), shape(own.shape, dtype), [vmem] * 2
        )(own, got)

    node_scale = 1.0 / math.sqrt(TILE * n_rows * n_cols)
    mask = 1
    while mask < n_rows:
        term_got, got = partner(term_send, mask), partner(send, mask)
        mask *= 2
        if mask == n_rows:
            term_got, got = lax.optimization_barrier((term_got, got))
        else:
            term = term_send = add(BF16, 1.0, term, term_got)
            rows = keep.shape[0] // 2
            keep, send = call(
                fold_kernel, (shape((rows, width), F32), shape((rows, width), BF16)), [vmem] * 2
            )(keep, got)
    term = add(F32, node_scale, term, term_got)
    weight_grad = call(join_kernel, shape((width, width), F32), [vmem] * 2)(
        term, partner(term, 1)
    )
    input_grad = call(last_kernel, block_shape, [vmem] * 4)(degree, weight, keep, got)
    return (activated, input_grad, weight_grad)


def solution(mesh):
    placed = (
        P(("groups", "rows", "cols"), None),
        P(("groups", "rows", "cols")),
        P(),
        P(("groups", "rows"), "cols", None, None),
        P(("groups", "rows"), "cols", None, None, None),
        P(("groups", "rows"), "cols"),
        P(("groups", "rows", "cols"), None),
    )
    return jax.shard_map(
        shards,
        mesh=mesh,
        in_specs=placed,
        out_specs=(
            P(("groups", "rows", "cols"), None),
            P(("groups", "rows", "cols"), None),
            P("groups", None),
        ),
        check_vma=False,
    )
```

```python
import functools
import math

import jax
import jax.numpy as jnp
from jax import lax
from jax.experimental import pallas as pl
from jax.experimental.pallas import tpu as pltpu
from jax.sharding import PartitionSpec as P

TILE = 128
DEG_ROWS = 16
BF16 = jnp.bfloat16
F32 = jnp.float32


def reverse_bits(value, bits):
    out = value & 0
    for bit in range(bits):
        out = out | (((value >> bit) & 1) << (bits - 1 - bit))
    return out


def row_scale(degree_lanes):
    spread = jnp.broadcast_to(degree_lanes.astype(F32), (TILE, TILE))
    return lax.rsqrt(spread.T)


def wide(scale, width):
    return jnp.concatenate([scale] * (width // TILE), axis=1)


def rows_at(block, rows=TILE):
    return pl.ds(pl.multiple_of(block * rows, rows), rows)


def scale_kernel(deg_ref, x_ref, out_ref):
    scale = wide(row_scale(deg_ref[...].reshape(1, TILE)), x_ref.shape[1])
    out_ref[...] = (scale * x_ref[...].astype(F32)).astype(BF16)


def extra_kernel(deg_ref, cot_ref, extra_ref):
    extra_ref[:TILE] = cot_ref[...]
    degree = jnp.broadcast_to(deg_ref[...].reshape(1, TILE).astype(F32), (DEG_ROWS, TILE))
    extra_ref[TILE:] = wide(degree, cot_ref.shape[1]).astype(BF16)


def place_tiles(idx_ref, cnt_ref, values_ref, out_ref, transposed, bits):
    row_me, col_me = lax.axis_index("rows"), lax.axis_index("cols")
    used = cnt_ref[0, 0]
    out_ref[...] = jnp.zeros_like(out_ref)
    for slot in range(values_ref.shape[2]):
        live = slot < used
        row = jnp.where(live, idx_ref[0, 0, 0, slot], 0) ^ col_me
        col = jnp.where(live, idx_ref[0, 0, 1, slot], 0) ^ row_me
        row = jnp.where(live, row, 0)
        col = jnp.where(live, col, 0)
        tile = jnp.where(live, values_ref[0, 0, slot], jnp.zeros((TILE, TILE), BF16))
        at = (row, col)
        if transposed:
            tile = tile.T
            at = (reverse_bits(col, bits), row)
        here = (rows_at(at[0]), rows_at(at[1]))
        out_ref[here] = (out_ref[here].astype(F32) + tile.astype(F32)).astype(BF16)


def block_kernel(transposed, bits, idx_ref, cnt_ref, values_ref, *rest):
    place_tiles(idx_ref, cnt_ref, values_ref, rest[-1], transposed, bits)


def forward_kernel(n_rows, n_cols, matrix_ref, *rest):
    blocks, outs, panel = rest[:n_rows], rest[n_rows : n_rows + n_cols], rest[-1]
    for shift, block in enumerate(blocks):
        panel[shift * TILE : (shift + 1) * TILE] = block[...]
    for shift, out in enumerate(outs):
        out[...] = jnp.dot(
            matrix_ref[shift * TILE : (shift + 1) * TILE, :],
            panel[...],
            preferred_element_type=F32,
        ).astype(BF16)


def own_rows_kernel(deg_ref, *rest):
    blocks, out_ref = rest[:-1], rest[-1]
    sums = blocks[0][...].astype(F32)
    for block in blocks[1:]:
        sums = sums + block[...].astype(F32)
    scale = wide(row_scale(deg_ref[...].reshape(1, TILE)), sums.shape[1])
    out_ref[...] = (scale * sums).astype(BF16)


def middle_kernel(n_rows, n_cols, weight_ref, matrix_ref, *rest):
    panels, extras = rest[:n_cols], rest[n_cols : 2 * n_cols]
    act_ref, keep_ref, term_ref, send_ref, spread, term = rest[2 * n_cols :]
    width = weight_ref.shape[0]
    weight = weight_ref[...]
    term[...] = jnp.zeros_like(term)
    for shift in range(n_cols):
        extra = extras[shift]
        scale = wide(row_scale(extra[TILE : TILE + 1, :TILE]), width)
        aggregated = panels[shift][...]
        pre_act = jnp.dot(aggregated, weight, preferred_element_type=F32)
        sig = 1.0 / (1.0 + jnp.exp(-pre_act))
        if shift == 0:
            act_ref[...] = (pre_act * sig).astype(BF16)
        grad = extra[:TILE, :].astype(F32) * sig * (1.0 + pre_act * (1.0 - sig))
        spread[shift * TILE : (shift + 1) * TILE] = (scale * grad).astype(BF16)
        term[...] += lax.dot_general(
            aggregated, grad.astype(BF16), (((0,), (0,)), ((), ())), preferred_element_type=F32
        )
    half_rows = n_rows // 2 * TILE
    for place in range(n_rows):
        here = slice(place * TILE, (place + 1) * TILE)
        hidden = jnp.dot(matrix_ref[here, :], spread[...], preferred_element_type=F32)
        if place < n_rows // 2:
            keep_ref[here] = hidden
        else:
            send_ref[place * TILE - half_rows : (place + 1) * TILE - half_rows] = hidden.astype(BF16)
    side = lax.rem(lax.axis_index("rows"), 2)
    half = width // 2
    term_ref[...] = term[rows_at(side, half), :]
    send_ref[half_rows:] = term[rows_at(1 - side, half), :].astype(BF16)


def fold_kernel(keep_ref, term_ref, got_ref, keep_out, term_out, send_out):
    rows = keep_ref.shape[0]
    half = rows // 2
    keep_out[...] = keep_ref[:half] + got_ref[:half].astype(F32)
    term = (term_ref[...].astype(F32) + got_ref[rows:].astype(F32)).astype(BF16)
    send_out[:half] = (keep_ref[half:] + got_ref[half:rows].astype(F32)).astype(BF16)
    send_out[half:] = term
    term_out[...] = term


def add_kernel(scale, own_ref, got_ref, out_ref):
    got = got_ref[got_ref.shape[0] - own_ref.shape[0] :]
    out_ref[...] = (own_ref[...].astype(F32) + got.astype(F32)) * scale


def join_kernel(own_ref, got_ref, out_ref):
    half = own_ref.shape[0]
    side = lax.rem(lax.axis_index("rows"), 2)
    out_ref[rows_at(side, half), :] = own_ref[...]
    out_ref[rows_at(1 - side, half), :] = got_ref[...]


def last_kernel(deg_ref, weight_ref, keep_ref, got_ref, grad_ref):
    hidden = (keep_ref[...] + got_ref[: keep_ref.shape[0]].astype(F32)).astype(BF16)
    back = lax.dot_general(
        hidden, weight_ref[...], (((1,), (1,)), ((), ())), preferred_element_type=F32
    )
    scale = wide(row_scale(deg_ref[...].reshape(1, TILE)), back.shape[1])
    grad_ref[...] = (scale * back).astype(BF16)


def call(body, out_shapes, places, scratch=(), cost=None):
    return pl.pallas_call(
        body,
        out_shape=out_shapes,
        in_specs=[pl.BlockSpec(memory_space=place) for place in places],
        scratch_shapes=list(scratch),
        cost_estimate=cost,
        compiler_params=pltpu.CompilerParams(vmem_limit_bytes=24 * 1024 * 1024),
    )


def shards(features, degree, weight, tile_index, tile_values, tile_count, cotangent):
    width = features.shape[1]
    n_rows = lax.axis_size("rows")
    n_cols = lax.axis_size("cols")
    shape = jax.ShapeDtypeStruct
    smem, vmem = pltpu.SMEM, pltpu.VMEM

    def shifted(block, axis, size):
        got = [block] + [None] * (size - 1)
        for shift in reversed(range(1, size)):
            source = block[shift] if isinstance(block, (list, tuple)) else block
            got[shift] = lax.ppermute(source, axis, [(i, i ^ shift) for i in range(size)])
        if isinstance(block, (list, tuple)):
            got[0] = block[0]
        return got

    block_shape = shape((TILE, width), BF16)
    slow = pl.CostEstimate(flops=10**10, bytes_accessed=10**6, transcendentals=0)
    scaled = call(scale_kernel, block_shape, [vmem] * 2, cost=slow)(degree, features)
    extra = call(extra_kernel, shape((TILE + DEG_ROWS, width), BF16), [vmem] * 2)(degree, cotangent)
    bits = n_rows.bit_length() - 1
    matrix = call(
        functools.partial(block_kernel, False, bits),
        shape((n_cols * TILE, n_rows * TILE), BF16),
        [smem, smem, vmem],
    )(tile_index, tile_count, tile_values)
    blocks = shifted(scaled, "rows", n_rows)
    extras = shifted(extra, "cols", n_cols)
    parts = call(
        functools.partial(forward_kernel, n_rows, n_cols),
        [block_shape] * n_cols,
        [vmem] * (1 + n_rows),
        [vmem((n_rows * TILE, width), BF16)],
        slow,
    )(matrix, *blocks)
    back_matrix = call(
        functools.partial(block_kernel, True, bits),
        shape((n_rows * TILE, n_cols * TILE), BF16),
        [smem, smem, vmem] + [pl.ANY],
    )(tile_index, tile_count, tile_values, parts[0])
    sums = shifted(parts, "cols", n_cols)
    sums, extras = lax.optimization_barrier((sums[::-1], extras))
    aggregated = call(own_rows_kernel, block_shape, [vmem] * (1 + n_cols))(degree, *sums)
    panels = shifted(aggregated, "cols", n_cols)
    half = n_rows // 2 * TILE
    side_rows = width // 2
    activated, keep, term, send = call(
        functools.partial(middle_kernel, n_rows, n_cols),
        (
            block_shape,
            shape((half, width), F32),
            shape((side_rows, width), F32),
            shape((half + side_rows, width), BF16),
        ),
        [vmem] * (2 + 2 * n_cols),
        [vmem((n_cols * TILE, width), BF16), vmem((width, width), F32)],
    )(weight, back_matrix, *panels, *extras)

    def partner(block, mask):
        return lax.ppermute(block, "rows", [(i, i ^ mask) for i in range(n_rows)])

    got = partner(send, 1)
    mask = 2
    while mask < n_rows:
        half = keep.shape[0] // 2
        keep, term, send = call(
            fold_kernel,
            (
                shape((half, width), F32),
                shape((side_rows, width), BF16),
                shape((half + side_rows, width), BF16),
            ),
            [vmem] * 3,
        )(keep, term, got)
        got = partner(send, mask)
        mask *= 2
    node_scale = 1.0 / math.sqrt(TILE * n_rows * n_cols)
    term = call(
        functools.partial(add_kernel, node_scale), shape((side_rows, width), F32), [vmem] * 2
    )(term, got)
    weight_grad = call(join_kernel, shape((width, width), F32), [vmem] * 2)(
        term, partner(term, 1)
    )
    input_grad = call(last_kernel, block_shape, [vmem] * 4)(degree, weight, keep, got)
    return (activated, input_grad, weight_grad)


def solution(mesh):
    placed = (
        P(("groups", "rows", "cols"), None),
        P(("groups", "rows", "cols")),
        P(),
        P(("groups", "rows"), "cols", None, None),
        P(("groups", "rows"), "cols", None, None, None),
        P(("groups", "rows"), "cols"),
        P(("groups", "rows", "cols"), None),
    )
    return jax.shard_map(
        shards,
        mesh=mesh,
        in_specs=placed,
        out_specs=(
            P(("groups", "rows", "cols"), None),
            P(("groups", "rows", "cols"), None),
            P("groups", None),
        ),
        check_vma=False,
    )
```

```python
import functools
import math

import jax
import jax.numpy as jnp
from jax import lax
from jax.experimental import pallas as pl
from jax.experimental.pallas import tpu as pltpu
from jax.sharding import PartitionSpec as P

TILE = 128
DEG_ROWS = 16
BF16 = jnp.bfloat16
F32 = jnp.float32


def reverse_bits(value, bits):
    out = value & 0
    for bit in range(bits):
        out = out | (((value >> bit) & 1) << (bits - 1 - bit))
    return out


def row_scale(degree_lanes):
    spread = jnp.broadcast_to(degree_lanes.astype(F32), (TILE, TILE))
    return lax.rsqrt(spread.T)


def wide(scale, width):
    return jnp.concatenate([scale] * (width // TILE), axis=1)


def rows_at(block, rows=TILE):
    return pl.ds(pl.multiple_of(block * rows, rows), rows)


def scale_kernel(deg_ref, x_ref, out_ref):
    scale = wide(row_scale(deg_ref[...].reshape(1, TILE)), x_ref.shape[1])
    out_ref[...] = (scale * x_ref[...].astype(F32)).astype(BF16)


def extra_kernel(deg_ref, cot_ref, extra_ref):
    width = cot_ref.shape[1]
    for at in range(0, width, TILE):
        extra_ref[at : at + TILE] = cot_ref[:, at : at + TILE]
    degree = jnp.broadcast_to(deg_ref[...].reshape(1, TILE).astype(F32), (DEG_ROWS, TILE))
    extra_ref[width:] = degree.astype(BF16)


def place_tiles(idx_ref, cnt_ref, values_ref, out_ref, transposed, bits):
    row_me, col_me = lax.axis_index("rows"), lax.axis_index("cols")
    used = cnt_ref[0, 0]
    out_ref[...] = jnp.zeros_like(out_ref)
    for slot in range(values_ref.shape[2]):
        live = slot < used
        row = jnp.where(live, idx_ref[0, 0, 0, slot], 0) ^ col_me
        col = jnp.where(live, idx_ref[0, 0, 1, slot], 0) ^ row_me
        row = jnp.where(live, row, 0)
        col = jnp.where(live, col, 0)
        tile = jnp.where(live, values_ref[0, 0, slot], jnp.zeros((TILE, TILE), BF16))
        at = (row, col)
        if transposed:
            tile = tile.T
            at = (reverse_bits(col, bits), row)
        here = (rows_at(at[0]), rows_at(at[1]))
        out_ref[here] = (out_ref[here].astype(F32) + tile.astype(F32)).astype(BF16)


def block_kernel(transposed, bits, idx_ref, cnt_ref, values_ref, *rest):
    place_tiles(idx_ref, cnt_ref, values_ref, rest[-1], transposed, bits)


def forward_kernel(n_rows, n_cols, matrix_ref, *rest):
    blocks, outs, panel = rest[:n_rows], rest[n_rows : n_rows + n_cols], rest[-1]
    for shift, block in enumerate(blocks):
        panel[shift * TILE : (shift + 1) * TILE] = block[...]
    for shift, out in enumerate(outs):
        out[...] = jnp.dot(
            matrix_ref[shift * TILE : (shift + 1) * TILE, :],
            panel[...],
            preferred_element_type=F32,
        ).astype(BF16)


def own_rows_kernel(deg_ref, *rest):
    blocks, out_ref = rest[:-1], rest[-1]
    sums = blocks[0][...].astype(F32)
    for block in blocks[1:]:
        sums = sums + block[...].astype(F32)
    scale = wide(row_scale(deg_ref[...].reshape(1, TILE)), sums.shape[1])
    out_ref[...] = (scale * sums).astype(BF16)


def middle_kernel(n_rows, n_cols, weight_ref, matrix_ref, *rest):
    panels, extras = rest[:n_cols], rest[n_cols : 2 * n_cols]
    act_ref, keep_ref, term_ref, send_ref, spread, term = rest[2 * n_cols :]
    width = weight_ref.shape[0]
    weight = weight_ref[...]
    term[...] = jnp.zeros_like(term)
    for shift in range(n_cols):
        extra = extras[shift]
        scale = wide(row_scale(extra[width : width + 1, :]), width)
        aggregated = panels[shift][...]
        pre_act = jnp.dot(aggregated, weight, preferred_element_type=F32)
        sig = 1.0 / (1.0 + jnp.exp(-pre_act))
        if shift == 0:
            act_ref[...] = (pre_act * sig).astype(BF16)
        cot = jnp.concatenate([extra[at : at + TILE] for at in range(0, width, TILE)], axis=1)
        grad = cot.astype(F32) * sig * (1.0 + pre_act * (1.0 - sig))
        spread[shift * TILE : (shift + 1) * TILE] = (scale * grad).astype(BF16)
        term[...] += lax.dot_general(
            aggregated, grad.astype(BF16), (((0,), (0,)), ((), ())), preferred_element_type=F32
        )
    half_rows = n_rows // 2 * TILE
    for place in range(n_rows):
        here = slice(place * TILE, (place + 1) * TILE)
        hidden = jnp.dot(matrix_ref[here, :], spread[...], preferred_element_type=F32)
        if place < n_rows // 2:
            keep_ref[here] = hidden
        else:
            send_ref[place * TILE - half_rows : (place + 1) * TILE - half_rows] = hidden.astype(BF16)
    side = lax.rem(lax.axis_index("rows"), 2)
    half = width // 2
    term_ref[...] = term[rows_at(side, half), :]
    send_ref[half_rows:] = term[rows_at(1 - side, half), :].astype(BF16)


def fold_kernel(keep_ref, term_ref, got_ref, keep_out, term_out, send_out):
    rows = keep_ref.shape[0]
    half = rows // 2
    keep_out[...] = keep_ref[:half] + got_ref[:half].astype(F32)
    term = (term_ref[...].astype(F32) + got_ref[rows:].astype(F32)).astype(BF16)
    send_out[:half] = (keep_ref[half:] + got_ref[half:rows].astype(F32)).astype(BF16)
    send_out[half:] = term
    term_out[...] = term


def add_kernel(scale, own_ref, got_ref, out_ref):
    got = got_ref[got_ref.shape[0] - own_ref.shape[0] :]
    out_ref[...] = (own_ref[...].astype(F32) + got.astype(F32)) * scale


def join_kernel(own_ref, got_ref, out_ref):
    half = own_ref.shape[0]
    side = lax.rem(lax.axis_index("rows"), 2)
    out_ref[rows_at(side, half), :] = own_ref[...]
    out_ref[rows_at(1 - side, half), :] = got_ref[...]


def last_kernel(deg_ref, weight_ref, keep_ref, got_ref, held_ref, grad_ref, act_ref):
    act_ref[...] = held_ref[...]
    hidden = (keep_ref[...] + got_ref[: keep_ref.shape[0]].astype(F32)).astype(BF16)
    back = lax.dot_general(
        hidden, weight_ref[...], (((1,), (1,)), ((), ())), preferred_element_type=F32
    )
    scale = wide(row_scale(deg_ref[...].reshape(1, TILE)), back.shape[1])
    grad_ref[...] = (scale * back).astype(BF16)


def call(body, out_shapes, places, scratch=(), cost=None):
    return pl.pallas_call(
        body,
        out_shape=out_shapes,
        in_specs=[pl.BlockSpec(memory_space=place) for place in places],
        scratch_shapes=list(scratch),
        cost_estimate=cost,
        compiler_params=pltpu.CompilerParams(vmem_limit_bytes=24 * 1024 * 1024),
    )


def shards(features, degree, weight, tile_index, tile_values, tile_count, cotangent):
    width = features.shape[1]
    n_rows = lax.axis_size("rows")
    n_cols = lax.axis_size("cols")
    shape = jax.ShapeDtypeStruct
    smem, vmem = pltpu.SMEM, pltpu.VMEM

    def shifted(block, axis, size):
        got = [block] + [None] * (size - 1)
        for shift in reversed(range(1, size)):
            source = block[shift] if isinstance(block, (list, tuple)) else block
            got[shift] = lax.ppermute(source, axis, [(i, i ^ shift) for i in range(size)])
        if isinstance(block, (list, tuple)):
            got[0] = block[0]
        return got

    block_shape = shape((TILE, width), BF16)
    slow = pl.CostEstimate(flops=10**10, bytes_accessed=10**6, transcendentals=0)
    scaled = call(scale_kernel, block_shape, [vmem] * 2, cost=slow)(degree, features)
    extra = call(extra_kernel, shape((width + DEG_ROWS, TILE), BF16), [vmem] * 2)(degree, cotangent)
    bits = n_rows.bit_length() - 1
    matrix = call(
        functools.partial(block_kernel, False, bits),
        shape((n_cols * TILE, n_rows * TILE), BF16),
        [smem, smem, vmem],
    )(tile_index, tile_count, tile_values)
    blocks = shifted(scaled, "rows", n_rows)
    def sent(block, shift):
        return lax.ppermute(block, "cols", [(j, j ^ shift) for j in range(n_cols)])

    late = [shift for shift in range(1, n_cols) if shift != 2]
    early = [shift for shift in range(1, n_cols) if shift == 2]
    extras = [extra] + [None] * (n_cols - 1)
    for shift in reversed(early):
        extras[shift] = sent(extra, shift)
    parts = call(
        functools.partial(forward_kernel, n_rows, n_cols),
        [block_shape] * n_cols,
        [vmem] * (1 + n_rows),
        [vmem((n_rows * TILE, width), BF16)],
        slow,
    )(matrix, *blocks)
    back_matrix = call(
        functools.partial(block_kernel, True, bits),
        shape((n_rows * TILE, n_cols * TILE), BF16),
        [smem, smem, vmem] + [pl.ANY],
    )(tile_index, tile_count, tile_values, parts[0])
    parts, tied = lax.optimization_barrier((parts, extra))
    for shift in reversed(late):
        extras[shift] = sent(tied, shift)
    sums = shifted(parts, "cols", n_cols)
    held = [extras[shift] for shift in early]
    sums, held = lax.optimization_barrier((sums[::-1], held))
    for shift, block in zip(early, held):
        extras[shift] = block
    aggregated = call(own_rows_kernel, block_shape, [vmem] * (1 + n_cols))(degree, *sums)
    panels = shifted(aggregated, "cols", n_cols)
    half = n_rows // 2 * TILE
    side_rows = width // 2
    kept_act, keep, term, send = call(
        functools.partial(middle_kernel, n_rows, n_cols),
        (
            block_shape,
            shape((half, width), F32),
            shape((side_rows, width), F32),
            shape((half + side_rows, width), BF16),
        ),
        [vmem] * (2 + 2 * n_cols),
        [vmem((n_cols * TILE, width), BF16), vmem((width, width), F32)],
    )(weight, back_matrix, *panels, *extras)

    def partner(block, mask):
        return lax.ppermute(block, "rows", [(i, i ^ mask) for i in range(n_rows)])

    got = partner(send, 1)
    mask = 2
    while mask < n_rows:
        half = keep.shape[0] // 2
        keep, term, send = call(
            fold_kernel,
            (
                shape((half, width), F32),
                shape((side_rows, width), BF16),
                shape((half + side_rows, width), BF16),
            ),
            [vmem] * 3,
        )(keep, term, got)
        got = partner(send, mask)
        mask *= 2
    node_scale = 1.0 / math.sqrt(TILE * n_rows * n_cols)
    term = call(
        functools.partial(add_kernel, node_scale), shape((side_rows, width), F32), [vmem] * 2
    )(term, got)
    weight_grad = call(join_kernel, shape((width, width), F32), [vmem] * 2)(
        term, partner(term, 1)
    )
    input_grad, activated = call(last_kernel, (block_shape, block_shape), [vmem] * 5)(
        degree, weight, keep, got, kept_act
    )
    return (activated, input_grad, weight_grad)


def solution(mesh):
    placed = (
        P(("groups", "rows", "cols"), None),
        P(("groups", "rows", "cols")),
        P(),
        P(("groups", "rows"), "cols", None, None),
        P(("groups", "rows"), "cols", None, None, None),
        P(("groups", "rows"), "cols"),
        P(("groups", "rows", "cols"), None),
    )
    return jax.shard_map(
        shards,
        mesh=mesh,
        in_specs=placed,
        out_specs=(
            P(("groups", "rows", "cols"), None),
            P(("groups", "rows", "cols"), None),
            P("groups", None),
        ),
        check_vma=False,
    )
```

```python
import functools
import math

import jax
import jax.numpy as jnp
from jax import lax
from jax.experimental import pallas as pl
from jax.experimental.pallas import tpu as pltpu
from jax.sharding import PartitionSpec as P

TILE = 128
DEG_ROWS = 16
BF16 = jnp.bfloat16
F32 = jnp.float32


def reverse_bits(value, bits):
    out = value & 0
    for bit in range(bits):
        out = out | (((value >> bit) & 1) << (bits - 1 - bit))
    return out


def row_scale(degree_lanes):
    spread = jnp.broadcast_to(degree_lanes.astype(F32), (TILE, TILE))
    return lax.rsqrt(spread.T)


def wide(scale, width):
    return jnp.concatenate([scale] * (width // TILE), axis=1)


def rows_at(block, rows=TILE):
    return pl.ds(pl.multiple_of(block * rows, rows), rows)


def scale_kernel(deg_ref, x_ref, out_ref):
    scale = wide(row_scale(deg_ref[...].reshape(1, TILE)), x_ref.shape[1])
    out_ref[...] = (scale * x_ref[...].astype(F32)).astype(BF16)


def extra_kernel(deg_ref, cot_ref, extra_ref):
    width = cot_ref.shape[1]
    for at in range(0, width, TILE):
        extra_ref[at : at + TILE] = cot_ref[:, at : at + TILE]
    degree = jnp.broadcast_to(deg_ref[...].reshape(1, TILE).astype(F32), (DEG_ROWS, TILE))
    extra_ref[width:] = degree.astype(BF16)


def place_tiles(idx_ref, cnt_ref, values_ref, out_ref, transposed, bits):
    row_me, col_me = lax.axis_index("rows"), lax.axis_index("cols")
    used = cnt_ref[0, 0]
    out_ref[...] = jnp.zeros_like(out_ref)
    for slot in range(values_ref.shape[2]):
        live = slot < used
        row = jnp.where(live, idx_ref[0, 0, 0, slot], 0) ^ col_me
        col = jnp.where(live, idx_ref[0, 0, 1, slot], 0) ^ row_me
        row = jnp.where(live, row, 0)
        col = jnp.where(live, col, 0)
        tile = jnp.where(live, values_ref[0, 0, slot], jnp.zeros((TILE, TILE), BF16))
        at = (row, col)
        if transposed:
            tile = tile.T
            at = (reverse_bits(col, bits), row)
        here = (rows_at(at[0]), rows_at(at[1]))
        out_ref[here] = (out_ref[here].astype(F32) + tile.astype(F32)).astype(BF16)


def block_kernel(transposed, bits, idx_ref, cnt_ref, values_ref, *rest):
    place_tiles(idx_ref, cnt_ref, values_ref, rest[-1], transposed, bits)


def forward_kernel(n_rows, n_cols, matrix_ref, *rest):
    blocks, outs, panel = rest[:n_rows], rest[n_rows : n_rows + n_cols], rest[-1]
    for shift, block in enumerate(blocks):
        panel[shift * TILE : (shift + 1) * TILE] = block[...]
    for shift, out in enumerate(outs):
        out[...] = jnp.dot(
            matrix_ref[shift * TILE : (shift + 1) * TILE, :],
            panel[...],
            preferred_element_type=F32,
        ).astype(BF16)


def own_rows_kernel(deg_ref, *rest):
    blocks, out_ref = rest[:-1], rest[-1]
    sums = blocks[0][...].astype(F32)
    for block in blocks[1:]:
        sums = sums + block[...].astype(F32)
    scale = wide(row_scale(deg_ref[...].reshape(1, TILE)), sums.shape[1])
    out_ref[...] = (scale * sums).astype(BF16)


def middle_kernel(n_rows, n_cols, weight_ref, matrix_ref, *rest):
    panels, extras = rest[:n_cols], rest[n_cols : 2 * n_cols]
    act_ref, keep_ref, term_ref, send_ref, spread, term = rest[2 * n_cols :]
    width = weight_ref.shape[0]
    weight = weight_ref[...]
    term[...] = jnp.zeros_like(term)
    for shift in range(n_cols):
        extra = extras[shift]
        scale = wide(row_scale(extra[width : width + 1, :]), width)
        aggregated = panels[shift][...]
        pre_act = jnp.dot(aggregated, weight, preferred_element_type=F32)
        sig = 1.0 / (1.0 + jnp.exp(-pre_act))
        if shift == 0:
            act_ref[...] = (pre_act * sig).astype(BF16)
        cot = jnp.concatenate([extra[at : at + TILE] for at in range(0, width, TILE)], axis=1)
        grad = cot.astype(F32) * sig * (1.0 + pre_act * (1.0 - sig))
        spread[shift * TILE : (shift + 1) * TILE] = (scale * grad).astype(BF16)
        term[...] += lax.dot_general(
            aggregated, grad.astype(BF16), (((0,), (0,)), ((), ())), preferred_element_type=F32
        )
    half_rows = n_rows // 2 * TILE
    for place in range(n_rows):
        here = slice(place * TILE, (place + 1) * TILE)
        hidden = jnp.dot(matrix_ref[here, :], spread[...], preferred_element_type=F32)
        if place < n_rows // 2:
            keep_ref[here] = hidden
        else:
            send_ref[place * TILE - half_rows : (place + 1) * TILE - half_rows] = hidden.astype(BF16)
    side = lax.rem(lax.axis_index("rows"), 2)
    half = width // 2
    term_ref[...] = term[rows_at(side, half), :]
    send_ref[half_rows:] = term[rows_at(1 - side, half), :].astype(BF16)


def fold_kernel(keep_ref, term_ref, got_ref, term_got_ref, keep_out, term_out, send_out):
    rows = keep_ref.shape[0]
    half = rows // 2
    term_got = term_got_ref[term_got_ref.shape[0] - term_ref.shape[0] :]
    keep_out[...] = keep_ref[:half] + got_ref[:half].astype(F32)
    term_out[...] = (term_ref[...].astype(F32) + term_got.astype(F32)).astype(BF16)
    send_out[...] = (keep_ref[half:] + got_ref[half:rows].astype(F32)).astype(BF16)


def add_kernel(scale, own_ref, got_ref, out_ref):
    got = got_ref[got_ref.shape[0] - own_ref.shape[0] :]
    out_ref[...] = ((own_ref[...].astype(F32) + got.astype(F32)) * scale).astype(out_ref.dtype)


def last_kernel(
    deg_ref, weight_ref, keep_ref, got_ref, held_ref, own_ref, other_ref, grad_ref, act_ref, wgrad_ref
):
    act_ref[...] = held_ref[...]
    hidden = (keep_ref[...] + got_ref[: keep_ref.shape[0]].astype(F32)).astype(BF16)
    back = lax.dot_general(
        hidden, weight_ref[...], (((1,), (1,)), ((), ())), preferred_element_type=F32
    )
    scale = wide(row_scale(deg_ref[...].reshape(1, TILE)), back.shape[1])
    grad_ref[...] = (scale * back).astype(BF16)
    half = own_ref.shape[0]
    side = lax.rem(lax.axis_index("rows"), 2)
    wgrad_ref[rows_at(side, half), :] = own_ref[...].astype(F32)
    wgrad_ref[rows_at(1 - side, half), :] = other_ref[...].astype(F32)


def call(body, out_shapes, places, scratch=(), cost=None):
    return pl.pallas_call(
        body,
        out_shape=out_shapes,
        in_specs=[pl.BlockSpec(memory_space=place) for place in places],
        scratch_shapes=list(scratch),
        cost_estimate=cost,
        compiler_params=pltpu.CompilerParams(vmem_limit_bytes=24 * 1024 * 1024),
    )


def shards(features, degree, weight, tile_index, tile_values, tile_count, cotangent):
    width = features.shape[1]
    n_rows = lax.axis_size("rows")
    n_cols = lax.axis_size("cols")
    shape = jax.ShapeDtypeStruct
    smem, vmem = pltpu.SMEM, pltpu.VMEM

    def shifted(block, axis, size):
        got = [block] + [None] * (size - 1)
        for shift in reversed(range(1, size)):
            source = block[shift] if isinstance(block, (list, tuple)) else block
            got[shift] = lax.ppermute(source, axis, [(i, i ^ shift) for i in range(size)])
        if isinstance(block, (list, tuple)):
            got[0] = block[0]
        return got

    block_shape = shape((TILE, width), BF16)
    slow = pl.CostEstimate(flops=10**10, bytes_accessed=10**6, transcendentals=0)
    scaled = call(scale_kernel, block_shape, [vmem] * 2, cost=slow)(degree, features)
    extra = call(extra_kernel, shape((width + DEG_ROWS, TILE), BF16), [vmem] * 2)(degree, cotangent)
    bits = n_rows.bit_length() - 1
    matrix = call(
        functools.partial(block_kernel, False, bits),
        shape((n_cols * TILE, n_rows * TILE), BF16),
        [smem, smem, vmem],
    )(tile_index, tile_count, tile_values)
    blocks = shifted(scaled, "rows", n_rows)
    def sent(block, shift):
        return lax.ppermute(block, "cols", [(j, j ^ shift) for j in range(n_cols)])

    late = [shift for shift in range(1, n_cols) if shift != 2]
    early = [shift for shift in range(1, n_cols) if shift == 2]
    extras = [extra] + [None] * (n_cols - 1)
    for shift in reversed(early):
        extras[shift] = sent(extra, shift)
    parts = call(
        functools.partial(forward_kernel, n_rows, n_cols),
        [block_shape] * n_cols,
        [vmem] * (1 + n_rows),
        [vmem((n_rows * TILE, width), BF16)],
        slow,
    )(matrix, *blocks)
    back_matrix = call(
        functools.partial(block_kernel, True, bits),
        shape((n_rows * TILE, n_cols * TILE), BF16),
        [smem, smem, vmem] + [pl.ANY],
    )(tile_index, tile_count, tile_values, parts[0])
    parts, tied = lax.optimization_barrier((parts, extra))
    for shift in reversed(late):
        extras[shift] = sent(tied, shift)
    sums = shifted(parts, "cols", n_cols)
    held = [extras[shift] for shift in early]
    sums, held = lax.optimization_barrier((sums[::-1], held))
    for shift, block in zip(early, held):
        extras[shift] = block
    aggregated = call(own_rows_kernel, block_shape, [vmem] * (1 + n_cols))(degree, *sums)
    panels = shifted(aggregated, "cols", n_cols)
    half = n_rows // 2 * TILE
    side_rows = width // 2
    kept_act, keep, term, send = call(
        functools.partial(middle_kernel, n_rows, n_cols),
        (
            block_shape,
            shape((half, width), F32),
            shape((side_rows, width), F32),
            shape((half + side_rows, width), BF16),
        ),
        [vmem] * (2 + 2 * n_cols),
        [vmem((n_cols * TILE, width), BF16), vmem((width, width), F32)],
    )(weight, back_matrix, *panels, *extras)

    def partner(block, mask):
        return lax.ppermute(block, "rows", [(i, i ^ mask) for i in range(n_rows)])

    got = term_got = partner(send, 1)
    mask = 2
    while mask < n_rows:
        half = keep.shape[0] // 2
        keep, term, send = call(
            fold_kernel,
            (
                shape((half, width), F32),
                shape((side_rows, width), BF16),
                shape((half, width), BF16),
            ),
            [vmem] * 4,
        )(keep, term, got, term_got)
        term_got, got = partner(term, mask), partner(send, mask)
        mask *= 2
    node_scale = 1.0 / math.sqrt(TILE * n_rows * n_cols)
    term = call(
        functools.partial(add_kernel, node_scale),
        shape((side_rows, width), BF16),
        [vmem] * 2,
        cost=slow,
    )(term, term_got)
    input_grad, activated, weight_grad = call(
        last_kernel, (block_shape, block_shape, shape((width, width), F32)), [vmem] * 7
    )(degree, weight, keep, got, kept_act, term, partner(term, 1))
    return (activated, input_grad, weight_grad)


def solution(mesh):
    placed = (
        P(("groups", "rows", "cols"), None),
        P(("groups", "rows", "cols")),
        P(),
        P(("groups", "rows"), "cols", None, None),
        P(("groups", "rows"), "cols", None, None, None),
        P(("groups", "rows"), "cols"),
        P(("groups", "rows", "cols"), None),
    )
    return jax.shard_map(
        shards,
        mesh=mesh,
        in_specs=placed,
        out_specs=(
            P(("groups", "rows", "cols"), None),
            P(("groups", "rows", "cols"), None),
            P("groups", None),
        ),
        check_vma=False,
    )
```

```python
import functools
import math

import jax
import jax.numpy as jnp
from jax import lax
from jax.experimental import pallas as pl
from jax.experimental.pallas import tpu as pltpu
from jax.sharding import PartitionSpec as P

TILE = 128
DEG_ROWS = 16
BF16 = jnp.bfloat16
F32 = jnp.float32


def reverse_bits(value, bits):
    out = value & 0
    for bit in range(bits):
        out = out | (((value >> bit) & 1) << (bits - 1 - bit))
    return out


def row_scale(degree_lanes):
    spread = jnp.broadcast_to(degree_lanes.astype(F32), (TILE, TILE))
    return lax.rsqrt(spread.T)


def wide(scale, width):
    return jnp.concatenate([scale] * (width // TILE), axis=1)


def rows_at(block, rows=TILE):
    return pl.ds(pl.multiple_of(block * rows, rows), rows)


def zero_kernel(out_ref):
    out_ref[...] = jnp.zeros_like(out_ref)


def scale_kernel(cnt_ref, zero_ref, deg_ref, x_ref, out_ref, used_ref):
    scale = wide(row_scale(deg_ref[...].reshape(1, TILE)), x_ref.shape[1])
    out_ref[...] = (scale * x_ref[...].astype(F32)).astype(BF16)
    used_ref[...] = zero_ref[...] + cnt_ref[0, 0]


def extra_kernel(deg_ref, cot_ref, extra_ref):
    width = cot_ref.shape[1]
    for at in range(0, width, TILE):
        extra_ref[at : at + TILE] = cot_ref[:, at : at + TILE]
    degree = jnp.broadcast_to(deg_ref[...].reshape(1, TILE).astype(F32), (DEG_ROWS, TILE))
    extra_ref[width:] = degree.astype(BF16)


def block_kernel(transposed, n_rows, n_cols, idx_ref, used_ref, values_ref, *rest):
    out_ref = rest[-1]
    row_me, col_me = lax.axis_index("rows"), lax.axis_index("cols")
    used = jnp.broadcast_to(used_ref[:1, :], (TILE, TILE))
    bits = n_rows.bit_length() - 1
    out_ref[...] = jnp.zeros_like(out_ref)
    for slot in range(values_ref.shape[2]):
        row = jnp.clip(idx_ref[0, 0, 0, slot], 0, n_cols - 1) ^ col_me
        col = jnp.clip(idx_ref[0, 0, 1, slot], 0, n_rows - 1) ^ row_me
        tile = jnp.where(slot < used, values_ref[0, 0, slot].astype(F32), 0.0)
        at = (row, col)
        if transposed:
            tile = tile.T
            at = (reverse_bits(col, bits), row)
        here = (rows_at(at[0]), rows_at(at[1]))
        out_ref[here] = (out_ref[here].astype(F32) + tile).astype(BF16)


def forward_kernel(n_rows, n_cols, matrix_ref, *rest):
    blocks, outs, panel = rest[:n_rows], rest[n_rows : n_rows + n_cols], rest[-1]
    for shift, block in enumerate(blocks):
        panel[shift * TILE : (shift + 1) * TILE] = block[...]
    for shift, out in enumerate(outs):
        out[...] = jnp.dot(
            matrix_ref[shift * TILE : (shift + 1) * TILE, :],
            panel[...],
            preferred_element_type=F32,
        ).astype(BF16)


def own_rows_kernel(deg_ref, *rest):
    blocks, out_ref = rest[:-1], rest[-1]
    sums = blocks[0][...].astype(F32)
    for block in blocks[1:]:
        sums = sums + block[...].astype(F32)
    scale = wide(row_scale(deg_ref[...].reshape(1, TILE)), sums.shape[1])
    out_ref[...] = (scale * sums).astype(BF16)


def middle_kernel(n_rows, n_cols, weight_ref, matrix_ref, *rest):
    panels, extras = rest[:n_cols], rest[n_cols : 2 * n_cols]
    act_ref, keep_ref, term_ref, send_ref, spread, term = rest[2 * n_cols :]
    width = weight_ref.shape[0]
    weight = weight_ref[...]
    term[...] = jnp.zeros_like(term)
    for shift in range(n_cols):
        extra = extras[shift]
        scale = wide(row_scale(extra[width : width + 1, :]), width)
        aggregated = panels[shift][...]
        pre_act = jnp.dot(aggregated, weight, preferred_element_type=F32)
        sig = 1.0 / (1.0 + jnp.exp(-pre_act))
        if shift == 0:
            act_ref[...] = (pre_act * sig).astype(BF16)
        cot = jnp.concatenate([extra[at : at + TILE] for at in range(0, width, TILE)], axis=1)
        grad = cot.astype(F32) * sig * (1.0 + pre_act * (1.0 - sig))
        spread[shift * TILE : (shift + 1) * TILE] = (scale * grad).astype(BF16)
        term[...] += lax.dot_general(
            aggregated, grad.astype(BF16), (((0,), (0,)), ((), ())), preferred_element_type=F32
        )
    half_rows = n_rows // 2 * TILE
    for place in range(n_rows):
        here = slice(place * TILE, (place + 1) * TILE)
        hidden = jnp.dot(matrix_ref[here, :], spread[...], preferred_element_type=F32)
        if place < n_rows // 2:
            keep_ref[here] = hidden
        else:
            send_ref[place * TILE - half_rows : (place + 1) * TILE - half_rows] = hidden.astype(BF16)
    side = lax.rem(lax.axis_index("rows"), 2)
    half = width // 2
    term_ref[...] = term[rows_at(side, half), :]
    send_ref[half_rows:] = term[rows_at(1 - side, half), :].astype(BF16)


def fold_kernel(keep_ref, term_ref, got_ref, term_got_ref, keep_out, term_out, send_out):
    rows = keep_ref.shape[0]
    half = rows // 2
    term_got = term_got_ref[term_got_ref.shape[0] - term_ref.shape[0] :]
    keep_out[...] = keep_ref[:half] + got_ref[:half].astype(F32)
    term_out[...] = (term_ref[...].astype(F32) + term_got.astype(F32)).astype(BF16)
    send_out[...] = (keep_ref[half:] + got_ref[half:rows].astype(F32)).astype(BF16)


def add_kernel(scale, own_ref, got_ref, out_ref):
    got = got_ref[got_ref.shape[0] - own_ref.shape[0] :]
    out_ref[...] = ((own_ref[...].astype(F32) + got.astype(F32)) * scale).astype(out_ref.dtype)


def last_kernel(
    deg_ref, weight_ref, keep_ref, got_ref, held_ref, own_ref, other_ref, grad_ref, act_ref, wgrad_ref
):
    act_ref[...] = held_ref[...]
    hidden = (keep_ref[...] + got_ref[: keep_ref.shape[0]].astype(F32)).astype(BF16)
    back = lax.dot_general(
        hidden, weight_ref[...], (((1,), (1,)), ((), ())), preferred_element_type=F32
    )
    scale = wide(row_scale(deg_ref[...].reshape(1, TILE)), back.shape[1])
    grad_ref[...] = (scale * back).astype(BF16)
    half = own_ref.shape[0]
    side = lax.rem(lax.axis_index("rows"), 2)
    wgrad_ref[rows_at(side, half), :] = own_ref[...].astype(F32)
    wgrad_ref[rows_at(1 - side, half), :] = other_ref[...].astype(F32)


def call(body, out_shapes, places, scratch=(), cost=None):
    return pl.pallas_call(
        body,
        out_shape=out_shapes,
        in_specs=[pl.BlockSpec(memory_space=place) for place in places],
        scratch_shapes=list(scratch),
        cost_estimate=cost,
        compiler_params=pltpu.CompilerParams(vmem_limit_bytes=24 * 1024 * 1024),
    )


def shards(features, degree, weight, tile_index, tile_values, tile_count, cotangent):
    width = features.shape[1]
    n_rows = lax.axis_size("rows")
    n_cols = lax.axis_size("cols")
    shape = jax.ShapeDtypeStruct
    smem, vmem = pltpu.SMEM, pltpu.VMEM

    def shifted(block, axis, size):
        got = [block] + [None] * (size - 1)
        for shift in reversed(range(1, size)):
            source = block[shift] if isinstance(block, (list, tuple)) else block
            got[shift] = lax.ppermute(source, axis, [(i, i ^ shift) for i in range(size)])
        if isinstance(block, (list, tuple)):
            got[0] = block[0]
        return got

    block_shape = shape((TILE, width), BF16)
    slow = pl.CostEstimate(flops=10**10, bytes_accessed=10**6, transcendentals=0)
    count_shape = shape((8, TILE), jnp.int32)
    zero = call(zero_kernel, count_shape, [], cost=slow)()
    scaled, used = call(
        scale_kernel, (block_shape, count_shape), [smem] + [vmem] * 3, cost=slow
    )(tile_count, zero, degree, features)
    extra = call(extra_kernel, shape((width + DEG_ROWS, TILE), BF16), [vmem] * 2)(degree, cotangent)
    matrix = call(
        functools.partial(block_kernel, False, n_rows, n_cols),
        shape((n_cols * TILE, n_rows * TILE), BF16),
        [smem, vmem, vmem],
    )(tile_index, used, tile_values)
    blocks = shifted(scaled, "rows", n_rows)
    def sent(block, shift):
        return lax.ppermute(block, "cols", [(j, j ^ shift) for j in range(n_cols)])

    late = [shift for shift in range(1, n_cols) if shift != 2]
    early = [shift for shift in range(1, n_cols) if shift == 2]
    extras = [extra] + [None] * (n_cols - 1)
    for shift in reversed(early):
        extras[shift] = sent(extra, shift)
    parts = call(
        functools.partial(forward_kernel, n_rows, n_cols),
        [block_shape] * n_cols,
        [vmem] * (1 + n_rows),
        [vmem((n_rows * TILE, width), BF16)],
        slow,
    )(matrix, *blocks)
    back_matrix = call(
        functools.partial(block_kernel, True, n_rows, n_cols),
        shape((n_rows * TILE, n_cols * TILE), BF16),
        [smem, vmem, vmem, pl.ANY],
    )(tile_index, used, tile_values, parts[0])
    sums = shifted(parts, "cols", n_cols)
    back_matrix, tied = lax.optimization_barrier((back_matrix, extra))
    for shift in reversed(late):
        extras[shift] = sent(tied, shift)
    held = [extras[shift] for shift in early]
    sums, held, back_matrix = lax.optimization_barrier((sums[::-1], held, back_matrix))
    for shift, block in zip(early, held):
        extras[shift] = block
    aggregated = call(own_rows_kernel, block_shape, [vmem] * (1 + n_cols))(degree, *sums)
    panels = shifted(aggregated, "cols", n_cols)
    half = n_rows // 2 * TILE
    side_rows = width // 2
    kept_act, keep, term, send = call(
        functools.partial(middle_kernel, n_rows, n_cols),
        (
            block_shape,
            shape((half, width), F32),
            shape((side_rows, width), F32),
            shape((half + side_rows, width), BF16),
        ),
        [vmem] * (2 + 2 * n_cols),
        [vmem((n_cols * TILE, width), BF16), vmem((width, width), F32)],
    )(weight, back_matrix, *panels, *extras)

    def partner(block, mask):
        return lax.ppermute(block, "rows", [(i, i ^ mask) for i in range(n_rows)])

    got = term_got = partner(send, 1)
    mask = 2
    while mask < n_rows:
        half = keep.shape[0] // 2
        keep, term, send = call(
            fold_kernel,
            (
                shape((half, width), F32),
                shape((side_rows, width), BF16),
                shape((half, width), BF16),
            ),
            [vmem] * 4,
        )(keep, term, got, term_got)
        term_got, got = partner(term, mask), partner(send, mask)
        mask *= 2
    node_scale = 1.0 / math.sqrt(TILE * n_rows * n_cols)
    term = call(
        functools.partial(add_kernel, node_scale),
        shape((side_rows, width), BF16),
        [vmem] * 2,
        cost=slow,
    )(term, term_got)
    input_grad, activated, weight_grad = call(
        last_kernel, (block_shape, block_shape, shape((width, width), F32)), [vmem] * 7
    )(degree, weight, keep, got, kept_act, term, partner(term, 1))
    return (activated, input_grad, weight_grad)


def solution(mesh):
    placed = (
        P(("groups", "rows", "cols"), None),
        P(("groups", "rows", "cols")),
        P(),
        P(("groups", "rows"), "cols", None, None),
        P(("groups", "rows"), "cols", None, None, None),
        P(("groups", "rows"), "cols"),
        P(("groups", "rows", "cols"), None),
    )
    return jax.shard_map(
        shards,
        mesh=mesh,
        in_specs=placed,
        out_specs=(
            P(("groups", "rows", "cols"), None),
            P(("groups", "rows", "cols"), None),
            P("groups", None),
        ),
        check_vma=False,
    )
```

```python
import functools
import math

import jax
import jax.numpy as jnp
from jax import lax
from jax.experimental import pallas as pl
from jax.experimental.pallas import tpu as pltpu
from jax.sharding import PartitionSpec as P

TILE = 128
DEG_ROWS = 16
BF16 = jnp.bfloat16
F32 = jnp.float32


def reverse_bits(value, bits):
    out = value & 0
    for bit in range(bits):
        out = out | (((value >> bit) & 1) << (bits - 1 - bit))
    return out


def row_scale(degree_lanes):
    spread = jnp.broadcast_to(degree_lanes.astype(F32), (TILE, TILE))
    return lax.rsqrt(spread.T)


def wide(scale, width):
    return jnp.concatenate([scale] * (width // TILE), axis=1)


def rows_at(block, rows=TILE):
    return pl.ds(pl.multiple_of(block * rows, rows), rows)


def zero_kernel(out_ref):
    out_ref[...] = jnp.zeros_like(out_ref)


def scale_kernel(cnt_ref, zero_ref, deg_ref, x_ref, out_ref, used_ref):
    scale = wide(row_scale(deg_ref[...].reshape(1, TILE)), x_ref.shape[1])
    out_ref[...] = (scale * x_ref[...].astype(F32)).astype(BF16)
    used_ref[...] = zero_ref[...] + cnt_ref[0, 0]


def extra_kernel(deg_ref, cot_ref, extra_ref):
    width = cot_ref.shape[1]
    for at in range(0, width, TILE):
        extra_ref[at : at + TILE] = cot_ref[:, at : at + TILE]
    degree = jnp.broadcast_to(deg_ref[...].reshape(1, TILE).astype(F32), (DEG_ROWS, TILE))
    extra_ref[width:] = degree.astype(BF16)


def block_kernel(transposed, n_rows, n_cols, idx_ref, used_ref, values_ref, *rest):
    out_ref = rest[-1]
    row_me, col_me = lax.axis_index("rows"), lax.axis_index("cols")
    used = jnp.broadcast_to(used_ref[:1, :], (TILE, TILE))
    bits = n_rows.bit_length() - 1
    out_ref[...] = jnp.zeros_like(out_ref)
    for slot in range(values_ref.shape[2]):
        row = jnp.clip(idx_ref[0, 0, 0, slot], 0, n_cols - 1) ^ col_me
        col = jnp.clip(idx_ref[0, 0, 1, slot], 0, n_rows - 1) ^ row_me
        tile = jnp.where(slot < used, values_ref[0, 0, slot].astype(F32), 0.0)
        at = (row, col)
        if transposed:
            tile = tile.T
            at = (reverse_bits(col, bits), row)
        here = (rows_at(at[0]), rows_at(at[1]))
        out_ref[here] = (out_ref[here].astype(F32) + tile).astype(BF16)


def forward_kernel(n_rows, n_cols, matrix_ref, *rest):
    blocks, outs, panel = rest[:n_rows], rest[n_rows : n_rows + n_cols], rest[-1]
    for shift, block in enumerate(blocks):
        panel[shift * TILE : (shift + 1) * TILE] = block[...]
    for shift, out in enumerate(outs):
        out[...] = jnp.dot(
            matrix_ref[shift * TILE : (shift + 1) * TILE, :],
            panel[...],
            preferred_element_type=F32,
        ).astype(BF16)


def own_rows_kernel(deg_ref, *rest):
    blocks, out_ref = rest[:-1], rest[-1]
    sums = blocks[0][...].astype(F32)
    for block in blocks[1:]:
        sums = sums + block[...].astype(F32)
    scale = wide(row_scale(deg_ref[...].reshape(1, TILE)), sums.shape[1])
    out_ref[...] = (scale * sums).astype(BF16)


def gradient_rows(panel, extra, weight):
    width = weight.shape[0]
    scale = wide(row_scale(extra[width : width + 1, :]), width)
    aggregated = panel[...]
    pre_act = jnp.dot(aggregated, weight, preferred_element_type=F32)
    sig = 1.0 / (1.0 + jnp.exp(-pre_act))
    cot = jnp.concatenate([extra[at : at + TILE] for at in range(0, width, TILE)], axis=1)
    grad = cot.astype(F32) * sig * (1.0 + pre_act * (1.0 - sig))
    term = lax.dot_general(
        aggregated, grad.astype(BF16), (((0,), (0,)), ((), ())), preferred_element_type=F32
    )
    return (pre_act * sig).astype(BF16), (scale * grad).astype(BF16), term


def middle_kernel(shifts, weight_ref, matrix_ref, *rest):
    panels, extras = rest[: len(shifts)], rest[len(shifts) : 2 * len(shifts)]
    act_ref, hidden_ref, term_ref, spread = rest[2 * len(shifts) :]
    weight = weight_ref[...]
    spread[...] = jnp.zeros_like(spread)
    term_ref[...] = jnp.zeros_like(term_ref)
    for shift, panel, extra in zip(shifts, panels, extras):
        activated, rows, term = gradient_rows(panel, extra, weight)
        if shift == 0:
            act_ref[...] = activated
        spread[shift * TILE : (shift + 1) * TILE] = rows
        term_ref[...] += term
    for at in range(0, hidden_ref.shape[0], TILE):
        hidden_ref[at : at + TILE] = jnp.dot(
            matrix_ref[at : at + TILE, :], spread[...], preferred_element_type=F32
        )


def finish_kernel(
    shift, weight_ref, matrix_ref, panel, extra, hidden_ref, sum_ref, keep_ref, term_ref, send_ref, total
):
    activated, rows, term = gradient_rows(panel, extra, weight_ref[...])
    half_rows = keep_ref.shape[0]
    for at in range(0, hidden_ref.shape[0], TILE):
        hidden = hidden_ref[at : at + TILE] + jnp.dot(
            matrix_ref[at : at + TILE, shift * TILE : (shift + 1) * TILE],
            rows,
            preferred_element_type=F32,
        )
        if at < half_rows:
            keep_ref[at : at + TILE] = hidden
        else:
            send_ref[at - half_rows : at - half_rows + TILE] = hidden.astype(BF16)
    total[...] = sum_ref[...] + term
    side = lax.rem(lax.axis_index("rows"), 2)
    half = total.shape[0] // 2
    term_ref[...] = total[rows_at(side, half), :]
    send_ref[half_rows:] = total[rows_at(1 - side, half), :].astype(BF16)


def fold_kernel(keep_ref, term_ref, got_ref, term_got_ref, keep_out, term_out, send_out):
    rows = keep_ref.shape[0]
    half = rows // 2
    term_got = term_got_ref[term_got_ref.shape[0] - term_ref.shape[0] :]
    keep_out[...] = keep_ref[:half] + got_ref[:half].astype(F32)
    term_out[...] = (term_ref[...].astype(F32) + term_got.astype(F32)).astype(BF16)
    send_out[...] = (keep_ref[half:] + got_ref[half:rows].astype(F32)).astype(BF16)


def add_kernel(scale, own_ref, got_ref, out_ref):
    got = got_ref[got_ref.shape[0] - own_ref.shape[0] :]
    out_ref[...] = ((own_ref[...].astype(F32) + got.astype(F32)) * scale).astype(out_ref.dtype)


def last_kernel(
    deg_ref, weight_ref, keep_ref, got_ref, held_ref, own_ref, other_ref, grad_ref, act_ref, wgrad_ref
):
    act_ref[...] = held_ref[...]
    hidden = (keep_ref[...] + got_ref[: keep_ref.shape[0]].astype(F32)).astype(BF16)
    back = lax.dot_general(
        hidden, weight_ref[...], (((1,), (1,)), ((), ())), preferred_element_type=F32
    )
    scale = wide(row_scale(deg_ref[...].reshape(1, TILE)), back.shape[1])
    grad_ref[...] = (scale * back).astype(BF16)
    half = own_ref.shape[0]
    side = lax.rem(lax.axis_index("rows"), 2)
    wgrad_ref[rows_at(side, half), :] = own_ref[...].astype(F32)
    wgrad_ref[rows_at(1 - side, half), :] = other_ref[...].astype(F32)


def call(body, out_shapes, places, scratch=(), cost=None):
    return pl.pallas_call(
        body,
        out_shape=out_shapes,
        in_specs=[pl.BlockSpec(memory_space=place) for place in places],
        scratch_shapes=list(scratch),
        cost_estimate=cost,
        compiler_params=pltpu.CompilerParams(vmem_limit_bytes=24 * 1024 * 1024),
    )


def shards(features, degree, weight, tile_index, tile_values, tile_count, cotangent):
    width = features.shape[1]
    n_rows = lax.axis_size("rows")
    n_cols = lax.axis_size("cols")
    shape = jax.ShapeDtypeStruct
    smem, vmem = pltpu.SMEM, pltpu.VMEM

    def shifted(block, axis, size):
        got = [block] + [None] * (size - 1)
        for shift in reversed(range(1, size)):
            source = block[shift] if isinstance(block, (list, tuple)) else block
            got[shift] = lax.ppermute(source, axis, [(i, i ^ shift) for i in range(size)])
        if isinstance(block, (list, tuple)):
            got[0] = block[0]
        return got

    block_shape = shape((TILE, width), BF16)
    slow = pl.CostEstimate(flops=10**10, bytes_accessed=10**6, transcendentals=0)
    count_shape = shape((8, TILE), jnp.int32)
    zero = call(zero_kernel, count_shape, [], cost=slow)()
    scaled, used = call(
        scale_kernel, (block_shape, count_shape), [smem] + [vmem] * 3, cost=slow
    )(tile_count, zero, degree, features)
    extra = call(extra_kernel, shape((width + DEG_ROWS, TILE), BF16), [vmem] * 2)(degree, cotangent)
    matrix = call(
        functools.partial(block_kernel, False, n_rows, n_cols),
        shape((n_cols * TILE, n_rows * TILE), BF16),
        [smem, vmem, vmem],
    )(tile_index, used, tile_values)
    blocks = shifted(scaled, "rows", n_rows)
    def sent(block, shift):
        return lax.ppermute(block, "cols", [(j, j ^ shift) for j in range(n_cols)])

    late = [shift for shift in range(1, n_cols) if shift != 2]
    early = [shift for shift in range(1, n_cols) if shift == 2]
    extras = [extra] + [None] * (n_cols - 1)
    for shift in reversed(early):
        extras[shift] = sent(extra, shift)
    parts = call(
        functools.partial(forward_kernel, n_rows, n_cols),
        [block_shape] * n_cols,
        [vmem] * (1 + n_rows),
        [vmem((n_rows * TILE, width), BF16)],
        slow,
    )(matrix, *blocks)
    back_matrix = call(
        functools.partial(block_kernel, True, n_rows, n_cols),
        shape((n_rows * TILE, n_cols * TILE), BF16),
        [smem, vmem, vmem, pl.ANY],
    )(tile_index, used, tile_values, parts[0])
    sums = shifted(parts, "cols", n_cols)
    back_matrix, tied = lax.optimization_barrier((back_matrix, extra))
    for shift in reversed(late):
        extras[shift] = sent(tied, shift)
    held = [extras[shift] for shift in early]
    sums, held, back_matrix = lax.optimization_barrier((sums[::-1], held, back_matrix))
    for shift, block in zip(early, held):
        extras[shift] = block
    aggregated = call(own_rows_kernel, block_shape, [vmem] * (1 + n_cols))(degree, *sums)
    panels = shifted(aggregated, "cols", n_cols)
    half = n_rows // 2 * TILE
    side_rows = width // 2
    last = n_cols // 2
    shifts = [shift for shift in range(n_cols) if shift != last]
    kept_act, hidden, total = call(
        functools.partial(middle_kernel, shifts),
        (block_shape, shape((n_rows * TILE, width), F32), shape((width, width), F32)),
        [vmem] * (2 + 2 * len(shifts)),
        [vmem((n_cols * TILE, width), BF16)],
    )(
        weight,
        back_matrix,
        *[panels[shift] for shift in shifts],
        *[extras[shift] for shift in shifts],
    )
    keep, term, send = call(
        functools.partial(finish_kernel, last),
        (
            shape((half, width), F32),
            shape((side_rows, width), F32),
            shape((half + side_rows, width), BF16),
        ),
        [vmem] * 6,
        [vmem((width, width), F32)],
    )(weight, back_matrix, panels[last], extras[last], hidden, total)

    def partner(block, mask):
        return lax.ppermute(block, "rows", [(i, i ^ mask) for i in range(n_rows)])

    got = term_got = partner(send, 1)
    mask = 2
    while mask < n_rows:
        half = keep.shape[0] // 2
        keep, term, send = call(
            fold_kernel,
            (
                shape((half, width), F32),
                shape((side_rows, width), BF16),
                shape((half, width), BF16),
            ),
            [vmem] * 4,
        )(keep, term, got, term_got)
        term_got, got = partner(term, mask), partner(send, mask)
        mask *= 2
    node_scale = 1.0 / math.sqrt(TILE * n_rows * n_cols)
    term = call(
        functools.partial(add_kernel, node_scale),
        shape((side_rows, width), BF16),
        [vmem] * 2,
        cost=slow,
    )(term, term_got)
    input_grad, activated, weight_grad = call(
        last_kernel, (block_shape, block_shape, shape((width, width), F32)), [vmem] * 7
    )(degree, weight, keep, got, kept_act, term, partner(term, 1))
    return (activated, input_grad, weight_grad)


def solution(mesh):
    placed = (
        P(("groups", "rows", "cols"), None),
        P(("groups", "rows", "cols")),
        P(),
        P(("groups", "rows"), "cols", None, None),
        P(("groups", "rows"), "cols", None, None, None),
        P(("groups", "rows"), "cols"),
        P(("groups", "rows", "cols"), None),
    )
    return jax.shard_map(
        shards,
        mesh=mesh,
        in_specs=placed,
        out_specs=(
            P(("groups", "rows", "cols"), None),
            P(("groups", "rows", "cols"), None),
            P("groups", None),
        ),
        check_vma=False,
    )
```

```python
import functools
import math

import jax
import jax.numpy as jnp
from jax import lax
from jax.experimental import pallas as pl
from jax.experimental.pallas import tpu as pltpu
from jax.sharding import PartitionSpec as P

TILE = 128
DEG_ROWS = 16
BF16 = jnp.bfloat16
F32 = jnp.float32


def reverse_bits(value, bits):
    out = value & 0
    for bit in range(bits):
        out = out | (((value >> bit) & 1) << (bits - 1 - bit))
    return out


def row_scale(degree_lanes):
    spread = jnp.broadcast_to(degree_lanes.astype(F32), (TILE, TILE))
    return lax.rsqrt(spread.T)


def wide(scale, width):
    return jnp.concatenate([scale] * (width // TILE), axis=1)


def rows_at(block, rows=TILE):
    return pl.ds(pl.multiple_of(block * rows, rows), rows)


def zero_kernel(out_ref):
    out_ref[...] = jnp.zeros_like(out_ref)


def scale_kernel(cnt_ref, zero_ref, deg_ref, x_ref, out_ref, used_ref):
    scale = wide(row_scale(deg_ref[...].reshape(1, TILE)), x_ref.shape[1])
    out_ref[...] = (scale * x_ref[...].astype(F32)).astype(BF16)
    used_ref[...] = zero_ref[...] + cnt_ref[0, 0]


def extra_kernel(deg_ref, cot_ref, extra_ref):
    width = cot_ref.shape[1]
    for at in range(0, width, TILE):
        extra_ref[at : at + TILE] = cot_ref[:, at : at + TILE]
    degree = jnp.broadcast_to(deg_ref[...].reshape(1, TILE).astype(F32), (DEG_ROWS, TILE))
    extra_ref[width:] = degree.astype(BF16)


def block_kernel(transposed, n_rows, n_cols, idx_ref, used_ref, values_ref, *rest):
    out_ref = rest[-1]
    row_me, col_me = lax.axis_index("rows"), lax.axis_index("cols")
    used = jnp.broadcast_to(used_ref[:1, :], (TILE, TILE))
    bits = n_rows.bit_length() - 1
    out_ref[...] = jnp.zeros_like(out_ref)
    for slot in range(values_ref.shape[2]):
        row = jnp.clip(idx_ref[0, 0, 0, slot], 0, n_cols - 1) ^ col_me
        col = jnp.clip(idx_ref[0, 0, 1, slot], 0, n_rows - 1) ^ row_me
        tile = jnp.where(slot < used, values_ref[0, 0, slot].astype(F32), 0.0)
        at = (row, col)
        if transposed:
            tile = tile.T
            at = (reverse_bits(col, bits), row)
        here = (rows_at(at[0]), rows_at(at[1]))
        out_ref[here] = (out_ref[here].astype(F32) + tile).astype(BF16)


def forward_kernel(n_rows, n_cols, matrix_ref, *rest):
    blocks, outs, panel = rest[:n_rows], rest[n_rows : n_rows + n_cols], rest[-1]
    for shift, block in enumerate(blocks):
        panel[shift * TILE : (shift + 1) * TILE] = block[...]
    for shift, out in enumerate(outs):
        out[...] = jnp.dot(
            matrix_ref[shift * TILE : (shift + 1) * TILE, :],
            panel[...],
            preferred_element_type=F32,
        ).astype(BF16)


def own_rows_kernel(deg_ref, *rest):
    blocks, out_ref = rest[:-1], rest[-1]
    sums = blocks[0][...].astype(F32)
    for block in blocks[1:]:
        sums = sums + block[...].astype(F32)
    scale = wide(row_scale(deg_ref[...].reshape(1, TILE)), sums.shape[1])
    out_ref[...] = (scale * sums).astype(BF16)


def gradient_rows(panel, extra, weight):
    width = weight.shape[0]
    scale = wide(row_scale(extra[width : width + 16, :][:1]), width)
    aggregated = panel[...]
    pre_act = jnp.dot(aggregated, weight, preferred_element_type=F32)
    sig = 1.0 / (1.0 + jnp.exp(-pre_act))
    cot = jnp.concatenate([extra[at : at + TILE] for at in range(0, width, TILE)], axis=1)
    grad = cot.astype(F32) * sig * (1.0 + pre_act * (1.0 - sig))
    term = lax.dot_general(
        aggregated, grad.astype(BF16), (((0,), (0,)), ((), ())), preferred_element_type=F32
    )
    return (pre_act * sig).astype(BF16), (scale * grad).astype(BF16), term


def middle_kernel(shifts, weight_ref, matrix_ref, *rest):
    panels, extras = rest[: len(shifts)], rest[len(shifts) : 2 * len(shifts)]
    act_ref, hidden_ref, term_ref, spread = rest[2 * len(shifts) :]
    weight = weight_ref[...]
    spread[...] = jnp.zeros_like(spread)
    term_ref[...] = jnp.zeros_like(term_ref)
    for shift, panel, extra in zip(shifts, panels, extras):
        activated, rows, term = gradient_rows(panel, extra, weight)
        if shift == 0:
            act_ref[...] = activated
        spread[shift * TILE : (shift + 1) * TILE] = rows
        term_ref[...] += term
    for at in range(0, hidden_ref.shape[0], TILE):
        hidden_ref[at : at + TILE] = jnp.dot(
            matrix_ref[at : at + TILE, :], spread[...], preferred_element_type=F32
        )


def finish_kernel(
    shift, weight_ref, matrix_ref, panel, extra, hidden_ref, sum_ref, keep_ref, term_ref, send_ref, total
):
    activated, rows, term = gradient_rows(panel, extra, weight_ref[...])
    half_rows = keep_ref.shape[0]
    for at in range(0, hidden_ref.shape[0], TILE):
        hidden = hidden_ref[at : at + TILE] + jnp.dot(
            matrix_ref[at : at + TILE, shift * TILE : (shift + 1) * TILE],
            rows,
            preferred_element_type=F32,
        )
        if at < half_rows:
            keep_ref[at : at + TILE] = hidden
        else:
            send_ref[at - half_rows : at - half_rows + TILE] = hidden.astype(BF16)
    total[...] = sum_ref[...] + term
    side = lax.rem(lax.axis_index("rows"), 2)
    half = total.shape[0] // 2
    term_ref[...] = total[rows_at(side, half), :]
    send_ref[half_rows:] = total[rows_at(1 - side, half), :].astype(BF16)


def fold_kernel(keep_ref, term_ref, got_ref, term_got_ref, keep_out, term_out, send_out):
    rows = keep_ref.shape[0]
    half = rows // 2
    term_got = term_got_ref[term_got_ref.shape[0] - term_ref.shape[0] :]
    keep_out[...] = keep_ref[:half] + got_ref[:half].astype(F32)
    term_out[...] = (term_ref[...].astype(F32) + term_got.astype(F32)).astype(BF16)
    send_out[...] = (keep_ref[half:] + got_ref[half:rows].astype(F32)).astype(BF16)


def add_kernel(scale, own_ref, got_ref, out_ref):
    got = got_ref[got_ref.shape[0] - own_ref.shape[0] :]
    out_ref[...] = ((own_ref[...].astype(F32) + got.astype(F32)) * scale).astype(out_ref.dtype)


def last_kernel(
    deg_ref, weight_ref, keep_ref, got_ref, held_ref, own_ref, other_ref, grad_ref, act_ref, wgrad_ref
):
    act_ref[...] = held_ref[...]
    hidden = (keep_ref[...] + got_ref[: keep_ref.shape[0]].astype(F32)).astype(BF16)
    back = lax.dot_general(
        hidden, weight_ref[...], (((1,), (1,)), ((), ())), preferred_element_type=F32
    )
    scale = wide(row_scale(deg_ref[...].reshape(1, TILE)), back.shape[1])
    grad_ref[...] = (scale * back).astype(BF16)
    half = own_ref.shape[0]
    side = lax.rem(lax.axis_index("rows"), 2)
    wgrad_ref[rows_at(side, half), :] = own_ref[...].astype(F32)
    wgrad_ref[rows_at(1 - side, half), :] = other_ref[...].astype(F32)


def call(body, out_shapes, places, scratch=(), cost=None):
    return pl.pallas_call(
        body,
        out_shape=out_shapes,
        in_specs=[pl.BlockSpec(memory_space=place) for place in places],
        scratch_shapes=list(scratch),
        cost_estimate=cost,
        compiler_params=pltpu.CompilerParams(vmem_limit_bytes=24 * 1024 * 1024),
    )


def shards(features, degree, weight, tile_index, tile_values, tile_count, cotangent):
    width = features.shape[1]
    n_rows = lax.axis_size("rows")
    n_cols = lax.axis_size("cols")
    shape = jax.ShapeDtypeStruct
    smem, vmem = pltpu.SMEM, pltpu.VMEM

    def shifted(block, axis, size):
        got = [block] + [None] * (size - 1)
        for shift in reversed(range(1, size)):
            source = block[shift] if isinstance(block, (list, tuple)) else block
            got[shift] = lax.ppermute(source, axis, [(i, i ^ shift) for i in range(size)])
        if isinstance(block, (list, tuple)):
            got[0] = block[0]
        return got

    block_shape = shape((TILE, width), BF16)
    slow = pl.CostEstimate(flops=10**10, bytes_accessed=10**6, transcendentals=0)
    count_shape = shape((8, TILE), jnp.int32)
    zero = call(zero_kernel, count_shape, [], cost=slow)()
    scaled, used = call(
        scale_kernel, (block_shape, count_shape), [smem] + [vmem] * 3, cost=slow
    )(tile_count, zero, degree, features)
    extra = call(extra_kernel, shape((width + DEG_ROWS, TILE), BF16), [vmem] * 2)(degree, cotangent)
    matrix = call(
        functools.partial(block_kernel, False, n_rows, n_cols),
        shape((n_cols * TILE, n_rows * TILE), BF16),
        [smem, vmem, vmem],
    )(tile_index, used, tile_values)
    blocks = [scaled] + [
        lax.ppermute(scaled, "rows", [(i, i ^ shift) for i in range(n_rows)])
        for shift in range(1, n_rows)
    ]
    def sent(block, shift):
        return lax.ppermute(block, "cols", [(j, j ^ shift) for j in range(n_cols)])

    extras = [extra] + [None] * (n_cols - 1)
    for shift in range(2, n_cols, 2):
        extras[shift] = sent(extra, shift)
    parts = call(
        functools.partial(forward_kernel, n_rows, n_cols),
        [block_shape] * n_cols,
        [vmem] * (1 + n_rows),
        [vmem((n_rows * TILE, width), BF16)],
        slow,
    )(matrix, *blocks)
    back_matrix = call(
        functools.partial(block_kernel, True, n_rows, n_cols),
        shape((n_rows * TILE, n_cols * TILE), BF16),
        [smem, vmem, vmem, pl.ANY],
    )(tile_index, used, tile_values, parts[0])
    sums = shifted(parts, "cols", n_cols)
    early = list(range(2, n_cols, 2))
    back_matrix, tied, held = lax.optimization_barrier(
        (back_matrix, extra, [extras[shift] for shift in early])
    )
    extras[1] = sent(tied, 1)
    for shift, block in zip(early, held):
        extras[shift + 1] = sent(block, 1)
    sums, held, back_matrix = lax.optimization_barrier((sums[::-1], held, back_matrix))
    for shift, block in zip(early, held):
        extras[shift] = block
    aggregated = call(own_rows_kernel, block_shape, [vmem] * (1 + n_cols))(degree, *sums)
    panels = shifted(aggregated, "cols", n_cols)
    half = n_rows // 2 * TILE
    side_rows = width // 2
    last = n_cols // 2
    shifts = [shift for shift in range(n_cols) if shift != last]
    kept_act, hidden, total = call(
        functools.partial(middle_kernel, shifts),
        (block_shape, shape((n_rows * TILE, width), F32), shape((width, width), F32)),
        [vmem] * (2 + 2 * len(shifts)),
        [vmem((n_cols * TILE, width), BF16)],
    )(
        weight,
        back_matrix,
        *[panels[shift] for shift in shifts],
        *[extras[shift] for shift in shifts],
    )
    keep, term, send = call(
        functools.partial(finish_kernel, last),
        (
            shape((half, width), F32),
            shape((side_rows, width), F32),
            shape((half + side_rows, width), BF16),
        ),
        [vmem] * 6,
        [vmem((width, width), F32)],
    )(weight, back_matrix, panels[last], extras[last], hidden, total)

    def partner(block, mask):
        return lax.ppermute(block, "rows", [(i, i ^ mask) for i in range(n_rows)])

    got = term_got = partner(send, 1)
    mask = 2
    while mask < n_rows:
        half = keep.shape[0] // 2
        keep, term, send = call(
            fold_kernel,
            (
                shape((half, width), F32),
                shape((side_rows, width), BF16),
                shape((half, width), BF16),
            ),
            [vmem] * 4,
        )(keep, term, got, term_got)
        term_got, got = partner(term, mask), partner(send, mask)
        mask *= 2
    node_scale = 1.0 / math.sqrt(TILE * n_rows * n_cols)
    term = call(
        functools.partial(add_kernel, node_scale),
        shape((side_rows, width), BF16),
        [vmem] * 2,
        cost=slow,
    )(term, term_got)
    input_grad, activated, weight_grad = call(
        last_kernel, (block_shape, block_shape, shape((width, width), F32)), [vmem] * 7
    )(degree, weight, keep, got, kept_act, term, partner(term, 1))
    return (activated, input_grad, weight_grad)


def solution(mesh):
    placed = (
        P(("groups", "rows", "cols"), None),
        P(("groups", "rows", "cols")),
        P(),
        P(("groups", "rows"), "cols", None, None),
        P(("groups", "rows"), "cols", None, None, None),
        P(("groups", "rows"), "cols"),
        P(("groups", "rows", "cols"), None),
    )
    return jax.shard_map(
        shards,
        mesh=mesh,
        in_specs=placed,
        out_specs=(
            P(("groups", "rows", "cols"), None),
            P(("groups", "rows", "cols"), None),
            P("groups", None),
        ),
        check_vma=False,
    )
```
